128 devices in a mesh: tm: 8 (over y, z_hi), space: 16 (over x, z_lo, core).
Axes of the slice: x: 4, y: 4, z: 4 (z_hi: 2, z_lo: 2; z = z_hi * 2 + z_lo), core: 2. Of those that a mesh axis runs over, the one named last changes fastest.
Arguments:
- adjoint_iterate: float32 [8, 64, 256, 256], P('tm', 'space'), may hold values from -6 to 6
- forward_states: float32 [8, 2, 64, 256, 256], P('tm', None, 'space'), may hold values from -6 to 6
- conductivity: float32 [64, 256, 256], P('space'), may hold values from 0.25 to 4
- coarse_rate: float32 [64, 256, 256], P('space'), may hold values from 0.0125 to 4
- terminal_adjoint: float32 [64, 256, 256], P('space'), may hold values from -6 to 6
- smallest_eig: float32 [1], replicated, may hold values from 0.5 to 2
- largest_eig: float32 [1], replicated, may hold values from 50 to 64
Outputs:
- adjoint_next: float32 [8, 64, 256, 256], P('tm', 'space')
- sensitivity: float32 [64, 256, 256], P('space')
The draws below stay inside these ranges and needn't reach their ends.
All inputs are finite; a program needn't handle non-finite values.
Results may differ from the reference program's by a relative error of at most 0.0001.
Values sent between devices are 32-bit elements; how exact they have to be, the bound alone decides.
No kernel may reach another device: no remote copies, remote signals or barrier semaphores. Data moves between devices by JAX's collectives and lax.ppermute only.
A program may use at most 128 MiB of HBM per device.

```python
import math
import jax
import jax.numpy as jnp

NX = 256
NY = 256
SWEEPS = 8
NZ = 64
NT = 8


def shard_levels(stream_key, extent, pieces, smallest, top_value):
    level, own = 1.0, jax.random.fold_in(stream_key, 6)
    for axis_at, blocks in pieces:
        steps = jnp.exp(jax.random.uniform(jax.random.fold_in(own, axis_at), (blocks,), jnp.float32, smallest / len(pieces), top_value / len(pieces)))
        level = level * jnp.repeat(steps, extent[axis_at] // blocks).reshape([-1 if axis == axis_at else 1 for axis in range(len(extent))])
    return level


def gaussian(rng, shape, width, most, split=(), held_as=jnp.bfloat16):
    result = jax.random.normal(rng, shape, jnp.float32) * width
    if len(split) > 0:
        result = shard_levels(rng, shape, split, -0.22, 0.18) * result
    return jnp.clip(result, min=-most, max=most).astype(held_as)


def setup_inputs(seed: int = 0) -> dict:
    splits = jax.random.split(jax.random.key(seed), 8)
    adjoint_iterate = gaussian(splits[0], (NT, NZ, NX, NY), 1.0, 6.0, ((0, 8), (1, 16)), jnp.float32)
    forward_states = gaussian(splits[1], (NT, 2, NZ, NX, NY), 1.0, 6.0, ((0, 8), (2, 16)), jnp.float32)
    conductivity = jnp.clip(jnp.exp(math.log(4.0) - 2.7725887 * jax.random.uniform(splits[2], (NZ, NX, NY), jnp.float32) ** shard_levels(splits[2], (NZ, NX, NY), ((0, 16),), -0.2, 0.2)), 0.25, 4.0)
    coarse_rate = jnp.clip(jnp.exp(math.log(4.0) - 5.768321 * jax.random.uniform(splits[3], (NZ, NX, NY), jnp.float32) ** shard_levels(splits[3], (NZ, NX, NY), ((0, 16),), -0.2, 0.2)), 0.0125, 4.0)
    terminal_adjoint = gaussian(splits[4], (NZ, NX, NY), 1.0, 6.0, ((0, 16),), jnp.float32)
    smallest_eig = jnp.clip(jax.random.uniform(splits[5], (1,), jnp.float32, 0.5, 2.0), 0.5, 2.0)
    largest_eig = jnp.clip(jax.random.uniform(splits[6], (1,), jnp.float32, 50.0, 64.0), 50.0, 64.0)
    return {"adjoint_iterate": adjoint_iterate, "forward_states": forward_states, "conductivity": conductivity, "coarse_rate": coarse_rate, "terminal_adjoint": terminal_adjoint, "smallest_eig": smallest_eig, "largest_eig": largest_eig}


time_step = 1.0
NEIGHBOUR_STEPS = ((1, 0, 0), (-1, 0, 0), (0, 1, 0), (0, -1, 0), (0, 0, 1), (0, 0, -1))


def stencil(field_ext, coef_ext):
    plane_count, row_count, column_count = field_ext.shape
    padded = jnp.pad(field_ext, ((0, 0), (1, 1), (1, 1)))
    coef_pad = jnp.pad(coef_ext, ((0, 0), (1, 1), (1, 1)))
    center = padded[1:-1, 1:-1, 1:-1]
    coef_mid = coef_pad[1:-1, 1:-1, 1:-1]
    total = jnp.zeros_like(center)
    for shift_z, shift_x, shift_y in NEIGHBOUR_STEPS:
        near = padded[1 + shift_z:plane_count - 1 + shift_z, 1 + shift_x:row_count + 1 + shift_x, 1 + shift_y:column_count + 1 + shift_y]
        coef_near = coef_pad[1 + shift_z:plane_count - 1 + shift_z, 1 + shift_x:row_count + 1 + shift_x, 1 + shift_y:column_count + 1 + shift_y]
        total = total + 0.5 * (coef_mid + coef_near) * (center - near)
    return center + time_step * total


def face_term(adjoint_ext, state_ext):
    plane_count, row_count, column_count = adjoint_ext.shape
    adj_pad = jnp.pad(adjoint_ext, ((0, 0), (1, 1), (1, 1)))
    state_pad = jnp.pad(state_ext, ((0, 0), (1, 1), (1, 1)))
    adj_mid = adj_pad[1:-1, 1:-1, 1:-1]
    state_mid = state_pad[1:-1, 1:-1, 1:-1]
    total = jnp.zeros_like(adj_mid)
    for shift_z, shift_x, shift_y in NEIGHBOUR_STEPS:
        adj_near = adj_pad[1 + shift_z:plane_count - 1 + shift_z, 1 + shift_x:row_count + 1 + shift_x, 1 + shift_y:column_count + 1 + shift_y]
        state_near = state_pad[1 + shift_z:plane_count - 1 + shift_z, 1 + shift_x:row_count + 1 + shift_x, 1 + shift_y:column_count + 1 + shift_y]
        total = total + (adj_mid - adj_near) * (state_mid - state_near)
    return -time_step * 0.5 * total


def pad_planes(field):
    return jnp.pad(field, ((1, 1), (0, 0), (0, 0)))


def chebyshev(rhs, operator, smallest_eig, largest_eig):
    low = smallest_eig[0]
    high = largest_eig[0]
    center = (high + low) / 2.0
    radius = (high - low) / 2.0
    scaled = center / radius
    ratio = 1.0 / scaled
    iterate = jnp.zeros_like(rhs)
    residual = rhs
    direction = rhs / center
    for sweep_index in range(SWEEPS):
        iterate = iterate + direction
        residual = residual - operator(direction)
        ratio_next = 1.0 / (2.0 * scaled - ratio)
        direction = ratio_next * ratio * direction + (2.0 * ratio_next / radius) * residual
        ratio = ratio_next
    return iterate + direction


def reference(adjoint_iterate, forward_states, conductivity, coarse_rate, terminal_adjoint, smallest_eig, largest_eig):
    coef_ext = pad_planes(conductivity)

    def operator(field):
        return stencil(pad_planes(field), coef_ext)

    def solve(rhs):
        return chebyshev(rhs, operator, smallest_eig, largest_eig)

    ends = jnp.concatenate([adjoint_iterate[1:], terminal_adjoint[None]], axis=0)
    sensitivity = jnp.zeros_like(conductivity)
    earlies = []
    for slab in range(NT):
        late = solve(ends[slab])
        sensitivity = sensitivity + face_term(pad_planes(late), pad_planes(forward_states[slab, 1]))
        early = solve(late)
        sensitivity = sensitivity + face_term(pad_planes(early), pad_planes(forward_states[slab, 0]))
        earlies.append(early)
    decay = jnp.exp(-coarse_rate)
    carry = jnp.zeros_like(conductivity)
    results = [None] * NT
    for slab in range(NT - 1, -1, -1):
        results[slab] = earlies[slab] + decay * carry
        carry = (earlies[slab] - adjoint_iterate[slab]) + decay * carry
    return jnp.stack(results), sensitivity
```

```python
import jax
import jax.numpy as jnp
from jax import lax
from jax.experimental import pallas as pl
from jax.experimental.pallas import tpu as pltpu
from jax.sharding import PartitionSpec as P

SWEEPS = 8
NT = 8
GROUP = 16
CHIPS = 8
PLANES = 4
ROWS = 16
NY = 256
LANES = 128
HALO = 9
EXT = ROWS + 2 * HALO
F32 = jnp.float32
ANY = pl.BlockSpec(memory_space=pl.ANY)
SMEM = pl.BlockSpec(memory_space=pltpu.SMEM)
VMEM = pl.BlockSpec(memory_space=pltpu.VMEM)
DMA = pltpu.SemaphoreType.DMA


def chain_chip(g):
    return g ^ ((g >> 1) & 1)


def chain_place(c):
    return 2 * chain_chip(c >> 1) + (c & 1)


def call(kernel, out_shape, in_specs, out_specs, scratch, megabytes=16, flops=0):
    return pl.pallas_call(
        kernel,
        out_shape=out_shape,
        in_specs=in_specs,
        out_specs=out_specs,
        scratch_shapes=scratch,
        compiler_params=pltpu.CompilerParams(vmem_limit_bytes=megabytes * 1024 * 1024),
        cost_estimate=pl.CostEstimate(flops=flops, bytes_accessed=2**22, transcendentals=0),
    )


def struct(*shape):
    return jax.ShapeDtypeStruct(shape, F32)


def run(todo):
    for copy in todo:
        copy.start()
    for copy in todo:
        copy.wait()


def by_chip(field):
    return field.reshape(PLANES, CHIPS, 2, ROWS, NY)


def pack_first(ids, adjoint, terminal, conductivity, same, other, other_k, sems):
    tm, core = ids[0], ids[2]

    def copies(source):
        source = by_chip(source)
        return [
            pltpu.make_async_copy(source.at[:, :, core], same, sems.at[0]),
            pltpu.make_async_copy(source.at[:, :, 1 - core], other, sems.at[1]),
            pltpu.make_async_copy(
                by_chip(conductivity).at[:, :, 1 - core], other_k, sems.at[2]
            ),
        ]

    @pl.when(tm == 0)
    def _():
        run(copies(terminal))

    @pl.when(tm != 0)
    def _():
        run(copies(adjoint.at[0]))


def pack_states_first(ids, states, rate, other, sems):
    core = ids[2]
    run(
        [
            pltpu.make_async_copy(
                by_chip(field).at[:, :, 1 - core], other.at[at], sems.at[at]
            )
            for at, field in enumerate((states.at[0, 1], states.at[0, 0], rate))
        ]
    )


def pack_conductivity(ids, conductivity, received, *refs):
    outs, sems = refs[:CHIPS], refs[CHIPS]
    chip, core = ids[1], ids[2]
    todo = []
    for step in range(CHIPS):
        place = chain_chip(chip ^ step)
        todo += [
            pltpu.make_async_copy(
                by_chip(conductivity).at[:, place, core], outs[step].at[core], sems.at[0, step]
            ),
            pltpu.make_async_copy(
                received.at[:, place], outs[step].at[1 - core], sems.at[1, step]
            ),
        ]
    run(todo)


def pack_adjoint(ids, same, other, *refs):
    outs, sems = refs[:CHIPS], refs[CHIPS]
    chip, core = ids[1], ids[2]
    todo = []
    for step in range(CHIPS):
        place = chain_chip(chip ^ step)
        todo += [
            pltpu.make_async_copy(same.at[:, place], outs[step].at[core], sems.at[0, step]),
            pltpu.make_async_copy(other.at[:, place], outs[step].at[1 - core], sems.at[1, step]),
        ]
    run(todo)


def pack_states(ids, states, rate, received, *refs):
    outs, sems = refs[:CHIPS], refs[CHIPS]
    chip, core = ids[1], ids[2]
    todo = []
    for step in range(CHIPS):
        place = chain_chip(chip ^ step)
        for at, field in enumerate((states.at[0, 1], states.at[0, 0], rate)):
            todo.append(
                pltpu.make_async_copy(
                    by_chip(field).at[:, place, core], outs[step].at[core, at], sems.at[at, step]
                )
            )
        todo.append(
            pltpu.make_async_copy(
                received.at[:, :, place], outs[step].at[1 - core], sems.at[3, step]
            )
        )
    run(todo)


def fetch_pieces(me, pieces, slots, sems):
    todo = []
    for step, piece in enumerate(pieces):
        every = (slice(None),) * (len(piece.shape) - 1)
        for half in range(2):
            todo.append(
                pltpu.make_async_copy(
                    piece.at[every + (pl.ds(half * LANES, LANES),)],
                    slots.at[half, me ^ step],
                    sems.at[half, step],
                )
            )
    run(todo)


def strided(flat, start, stride):
    return jnp.concatenate(
        [flat[half][pl.ds(start, 8, stride=stride), :] for half in range(2)], axis=1
    )


def halves(slots):
    size = 1
    for extent in slots.shape[1:-1]:
        size *= extent
    return [slots.at[half].reshape(size, LANES) for half in range(2)]


def unpack_field(halo):
    def kernel(ids, *refs):
        pieces = refs[:CHIPS]
        own, up, down, slots, sems = refs[CHIPS:]
        fetch_pieces(ids[1], pieces, slots, sems)
        flat = halves(slots)

        def one_row(row, carry):
            for i in range(8):
                own[row, i] = strided(flat, i * ROWS + row, 8 * ROWS)
            return carry

        lax.fori_loop(0, ROWS, one_row, 0)
        up[...] = own[0:halo]
        down[...] = own[ROWS - halo :]

    return kernel


def unpack_states(ids, *refs):
    pieces = refs[:CHIPS]
    own, decay, up, down, slots, sems = refs[CHIPS:]
    fetch_pieces(ids[1], pieces, slots, sems)
    flat = halves(slots)

    def one_row(row, carry):
        for i in range(8):
            for field in range(3):
                start = (((i // PLANES) * 3 + field) * PLANES + i % PLANES) * ROWS + row
                lines = strided(flat, start, 6 * PLANES * ROWS)
                if field < 2:
                    own[field, row, i] = lines
                else:
                    decay[row, i] = jnp.exp(-lines)
        return carry

    lax.fori_loop(0, ROWS, one_row, 0)
    up[...] = own[:, 0]
    down[...] = own[:, ROWS - 1]


def coefficients(k, kx, ky, kw, kz, diag):
    lane = lax.broadcasted_iota(jnp.int32, (8, NY), 1)
    place = lax.broadcasted_iota(jnp.int32, (8, NY), 0)

    def one_row(e, carry):
        mids = [k[e, i] for i in range(8)]
        last = pltpu.roll(mids[7], 1, 0)
        after = pltpu.roll(mids[0], 7, 0)
        zs = [jnp.where(place == 0, 0.0, 0.5 * (mids[0] + last))]
        zs += [0.5 * (mids[i] + mids[i - 1]) for i in range(1, 8)]
        edge = (lane == 0) | (lane == NY - 1)
        done = []
        for i in range(8):
            mid = mids[i]
            before = jnp.where(lane == 0, 0.0, 0.5 * (mid + pltpu.roll(mid, 1, 1)))
            behind = jnp.where(lane == NY - 1, 0.0, 0.5 * (mid + pltpu.roll(mid, NY - 1, 1)))
            x_low = 0.5 * (mid + k[e - 1, i])
            x_high = 0.5 * (mid + k[e + 1, i])
            extra = jnp.where(edge, 0.5 * mid, 0.0)
            if i == 0:
                extra = extra + jnp.where(place == 0, 0.5 * mid, 0.0)
            if i == 7:
                extra = extra + jnp.where(place == 7, 0.5 * mid, 0.0)
            done.append((x_low, before, behind, 1.0 + extra + (before + behind) + (x_low + x_high)))
        for i in range(8):
            kx[e, i], ky[e, i], kw[e, i], diag[e, i] = done[i]
            kz[e, i] = zs[i]
        return carry

    lax.fori_loop(1, EXT - 1, one_row, 0)
    for i in range(8):
        kx[EXT - 1, i] = 0.5 * (k[EXT - 2, i] + k[EXT - 1, i])


def sweeps(ids, first, weights, d0, d1, r, x, kx, ky, kw, kz, diag):
    at = 2 * chain_chip(ids[1]) + ids[2]
    low = jnp.where(at == 0, HALO, 0)
    high = jnp.where(at == GROUP - 1, HALO + ROWS, EXT)
    start_weight = weights[0]

    def opening(e, carry):
        for i in range(8):
            rhs = d0[e, i]
            r[e, i] = rhs
            begin = rhs * start_weight
            d0[e, i] = begin
            x[e, i] = begin
        return carry

    lax.fori_loop(first, EXT - first, opening, 0)
    zeros = jnp.zeros((8, 8, NY), F32)
    d1[HALO - 1] = zeros
    d1[HALO + ROWS] = zeros

    def one_sweep(step, cur, nxt):
        alpha = weights[1 + 2 * step]
        beta = weights[2 + 2 * step]

        def one_row(e, inner):
            v = [cur[e, i] for i in range(8)]
            head = kz[e, 0] * (v[0] - pltpu.roll(v[7], 1, 0))
            tail = pltpu.roll(head, 7, 0)
            flux = head
            done = []
            for i in range(8):
                mid = v[i]
                flux_next = kz[e, i + 1] * (v[i + 1] - mid) if i < 7 else tail
                total = (
                    diag[e, i] * mid
                    + (flux - flux_next)
                    - kx[e, i] * cur[e - 1, i]
                    - kx[e + 1, i] * cur[e + 1, i]
                    - ky[e, i] * pltpu.roll(mid, 1, 1)
                    - kw[e, i] * pltpu.roll(mid, NY - 1, 1)
                )
                left = r[e, i] - total
                new = alpha * mid + beta * left
                r[e, i] = left
                nxt[e, i] = new
                x[e, i] = x[e, i] + new
                flux = flux_next
            return inner

        begin = jnp.maximum(first + step + 1, low)
        end = jnp.minimum(EXT - first - step - 1, high)

        def some_rows(n, inner):
            for extra in range(4):
                one_row(begin + 4 * n + extra, inner)
            return inner

        full = lax.div(end - begin, 4)
        lax.fori_loop(0, full, some_rows, 0)
        lax.fori_loop(begin + 4 * full, end, one_row, 0)

    def two_sweeps(pair, carry):
        one_sweep(2 * pair, d0, d1)
        one_sweep(2 * pair + 1, d1, d0)
        return carry

    lax.fori_loop(0, SWEEPS // 2, two_sweeps, 0)


FIELD = (EXT, 8, 8, NY)
SOLVE_SCRATCH = [pltpu.VMEM(FIELD, F32) for _ in range(10)] + [DMA((6,)), DMA((3,))]


def solve(halo):
    first = HALO - halo
    last = EXT - first

    def kernel(ids, weights, own_k, above_k, below_k, own, above, below, *refs):
        outs = refs[:-12]
        k, kx, ky, kw, kz, diag, r, x, d0, d1, sems, out_sems = refs[-12:]
        mine = pl.ds(HALO, ROWS)
        fields = [
            pltpu.make_async_copy(above_k, k.at[pl.ds(0, HALO)], sems.at[0]),
            pltpu.make_async_copy(own_k, k.at[mine], sems.at[1]),
            pltpu.make_async_copy(below_k, k.at[pl.ds(HALO + ROWS, HALO)], sems.at[2]),
        ]
        sides = [
            pltpu.make_async_copy(above, d0.at[pl.ds(first, halo)], sems.at[3]),
            pltpu.make_async_copy(own, d0.at[mine], sems.at[4]),
            pltpu.make_async_copy(below, d0.at[pl.ds(HALO + ROWS, halo)], sems.at[5]),
        ]
        for copy in fields + sides:
            copy.start()
        for copy in fields:
            copy.wait()
        coefficients(k, kx, ky, kw, kz, diag)
        for copy in sides:
            copy.wait()
        sweeps(ids, first, weights, d0, d1, r, x, kx, ky, kw, kz, diag)
        if halo == HALO:
            todo = [pltpu.make_async_copy(x.at[pl.ds(HALO - 1, ROWS + 2)], outs[0], out_sems.at[0])]
        else:
            todo = [
                pltpu.make_async_copy(x.at[mine], outs[0], out_sems.at[0]),
                pltpu.make_async_copy(x.at[pl.ds(HALO, HALO)], outs[1], out_sems.at[1]),
                pltpu.make_async_copy(x.at[pl.ds(ROWS, HALO)], outs[2], out_sems.at[2]),
            ]
        run(todo)

    return kernel


def face_rows(w, u, field, out, at, add):
    lane = lax.broadcasted_iota(jnp.int32, (8, NY), 1)
    place = lax.broadcasted_iota(jnp.int32, (8, NY), 0)

    def one_row(row, carry):
        e = row + 1
        vw = [w[e, i] for i in range(8)]
        vu = [u[field, row + 1, i] for i in range(8)]
        back_w = jnp.where(place == 0, 0.0, pltpu.roll(vw[7], 1, 0))
        back_u = jnp.where(place == 0, 0.0, pltpu.roll(vu[7], 1, 0))
        head = (vw[0] - back_w) * (vu[0] - back_u)
        face = head
        for i in range(8):
            if i < 7:
                face_next = (vw[i + 1] - vw[i]) * (vu[i + 1] - vu[i])
            else:
                face_next = jnp.where(place == 7, vw[7] * vu[7], pltpu.roll(head, 7, 0))
            side_w = jnp.where(lane == 0, 0.0, pltpu.roll(vw[i], 1, 1))
            side_u = jnp.where(lane == 0, 0.0, pltpu.roll(vu[i], 1, 1))
            face_y = (vw[i] - side_w) * (vu[i] - side_u)
            far_y = jnp.where(lane == NY - 1, vw[i] * vu[i], pltpu.roll(face_y, NY - 1, 1))
            total = (
                (face + face_next)
                + (face_y + far_y)
                + (vw[i] - w[e - 1, i]) * (vu[i] - u[field, row, i])
                + (vw[i] - w[e + 1, i]) * (vu[i] - u[field, row + 2, i])
            )
            total = -0.5 * total
            for half in range(2):
                part = total[:, half * LANES : (half + 1) * LANES]
                if add:
                    part = out[half, at, row, i] + part
                out[half, at, row, i] = part
            face = face_next
        return carry

    lax.fori_loop(0, ROWS, one_row, 0)


def face_sums(
    ids,
    late,
    late_above,
    late_below,
    early,
    states,
    states_above,
    states_below,
    decay,
    ends,
    *refs,
):
    outs = refs[:NT]
    w, x, u, rate_in, ends_in, pair, parts, sems, out_sems = refs[NT:]
    tm = ids[0]
    inner = pl.ds(1, ROWS)
    todo = [
        pltpu.make_async_copy(late_above.at[HALO - 1], w.at[0], sems.at[0]),
        pltpu.make_async_copy(late, w.at[inner], sems.at[1]),
        pltpu.make_async_copy(late_below.at[0], w.at[ROWS + 1], sems.at[2]),
        pltpu.make_async_copy(states_above, u.at[:, 0], sems.at[3]),
        pltpu.make_async_copy(states, u.at[:, inner], sems.at[4]),
        pltpu.make_async_copy(states_below, u.at[:, ROWS + 1], sems.at[5]),
        pltpu.make_async_copy(early, x, sems.at[6]),
        pltpu.make_async_copy(decay, rate_in, sems.at[7]),
        pltpu.make_async_copy(ends, ends_in, sems.at[8]),
    ]
    run(todo)
    face_rows(w, u, 0, pair, 1, False)
    face_rows(x, u, 1, pair, 1, True)
    keep = jnp.where(tm == NT - 1, 0.0, 1.0)

    def last_row(row, carry):
        for i in range(8):
            value = x[row + 1, i] - keep * (rate_in[row, i] * ends_in[row, i])
            for half in range(2):
                pair[half, 0, row, i] = value[:, half * LANES : (half + 1) * LANES]
        return carry

    lax.fori_loop(0, ROWS, last_row, 0)
    lines = halves(pair)

    def split_row(row, carry):
        for place in range(8):
            for field in range(2):
                start = (field * ROWS + row) * 64 + place
                parts[place, field, row] = strided(lines, start, 8)
        return carry

    lax.fori_loop(0, ROWS, split_row, 0)
    run(
        [
            pltpu.make_async_copy(parts.at[tm ^ step], outs[step], out_sems.at[step])
            for step in range(NT)
        ]
    )


def recur(ids, rate, received, *refs):
    pieces = refs[:NT]
    mine, other, slots, rates, results, sems, out_sems = refs[NT:]
    tm, chip, core = ids[0], ids[1], ids[2]
    place = chain_chip(tm)
    copies = [
        pltpu.make_async_copy(by_chip(rate).at[:, place, core], rates.at[core], out_sems.at[0]),
        pltpu.make_async_copy(received.at[2, :, place], rates.at[1 - core], out_sems.at[1]),
    ]
    for copy in copies:
        copy.start()
    fetch_pieces(chip, pieces, slots, sems)
    for copy in copies:
        copy.wait()
    flat = halves(slots)
    for side in range(2):
        for p in range(8):
            q, plane = p // PLANES, p % PLANES
            rows = pl.ds(8 * side, 8)

            def lines(slab, field):
                start = ((slab * 2 + field) * ROWS + 8 * side) * 8 + p
                return strided(flat, start, 8)

            decay = jnp.exp(-rates[q, plane, rows, :])
            value = lines(NT - 1, 0)
            results[q, NT - 1, plane, rows, :] = value
            for slab in range(NT - 2, -1, -1):
                value = lines(slab, 0) + decay * value
                results[q, slab, plane, rows, :] = value
            summed = lines(0, 1)
            for slab in range(1, NT):
                summed = summed + lines(slab, 1)
            results[q, NT, plane, rows, :] = summed
    run(
        [
            pltpu.make_async_copy(results.at[core], mine, out_sems.at[0]),
            pltpu.make_async_copy(results.at[1 - core], other, out_sems.at[1]),
        ]
    )


def pack_results(ids, mine, received, *refs):
    outs, sems = refs[:NT], refs[NT]
    tm, core = ids[0], ids[2]
    todo = []
    for step in range(NT):
        for field, at in enumerate((tm ^ step, NT)):
            for side, source in ((core, mine), (1 - core, received)):
                rows = pl.ds(pl.multiple_of(ROWS * side, ROWS), ROWS)
                todo.append(
                    pltpu.make_async_copy(
                        source.at[at], outs[step].at[field, :, rows, :], sems.at[len(todo)]
                    )
                )
    run(todo)


def place_results(ids, *refs):
    pieces = refs[:NT]
    adjoint, sensitivity, sems = refs[NT:]
    todo = []
    for step, piece in enumerate(pieces):
        row = pl.multiple_of(chain_chip(ids[0] ^ step) * 2 * ROWS, 2 * ROWS)
        rows = pl.ds(row, 2 * ROWS)
        todo += [
            pltpu.make_async_copy(piece.at[0], adjoint.at[0, :, rows, :], sems.at[0, step]),
            pltpu.make_async_copy(piece.at[1], sensitivity.at[:, rows, :], sems.at[1, step]),
        ]
    run(todo)


def sweep_weights(smallest_eig, largest_eig):
    low, high = smallest_eig[0], largest_eig[0]
    center = (high + low) / 2.0
    radius = (high - low) / 2.0
    scaled = center / radius
    ratio = 1.0 / scaled
    weights = [1.0 / center]
    for _ in range(SWEEPS):
        ratio_next = 1.0 / (2.0 * scaled - ratio)
        weights += [ratio_next * ratio, 2.0 * ratio_next / radius]
        ratio = ratio_next
    return jnp.stack(weights)


def per_device(
    adjoint_iterate,
    forward_states,
    conductivity,
    coarse_rate,
    terminal_adjoint,
    smallest_eig,
    largest_eig,
):
    here = lax.axis_index("space")
    ids = jnp.stack([lax.axis_index("tm"), here // 2, here % 2]).astype(jnp.int32)
    weights = sweep_weights(smallest_eig, largest_eig)
    both = ("tm", "space")
    earlier = [
        [
            (t * GROUP + c, ((t - 1) % NT) * GROUP + (c ^ swap))
            for t in range(NT)
            for c in range(GROUP)
        ]
        for swap in range(2)
    ]
    masks = [[(c, c ^ mask) for c in range(GROUP)] for mask in range(GROUP)]
    forward = [(chain_place(i), chain_place(i + 1)) for i in range(GROUP - 1)]
    backward = [(b, a) for a, b in forward]

    def to_chips(pieces):
        return [pieces[0]] + [
            lax.ppermute(pieces[step], "space", masks[2 * step]) for step in range(1, CHIPS)
        ]

    def along_chain(up, down):
        return lax.ppermute(down, "space", forward), lax.ppermute(up, "space", backward)

    part = (PLANES, CHIPS, ROWS, NY)
    block = (ROWS, 8, 8, NY)
    same, other, other_k = call(
        pack_first, [struct(*part)] * 3, [SMEM] + [ANY] * 3, [VMEM] * 3, [DMA((3,))], 56
    )(ids, adjoint_iterate, terminal_adjoint, conductivity)
    same = lax.ppermute(same, both, earlier[0])
    other = lax.ppermute(other, both, earlier[1])
    other_k = lax.ppermute(other_k, "space", masks[1])

    piece = struct(2, PLANES, ROWS, NY)
    pieces = call(
        pack_conductivity, [piece] * CHIPS, [SMEM, ANY, ANY], [VMEM] * CHIPS, [DMA((2, CHIPS))], 56
    )(ids, conductivity, other_k)

    def unpack(pieces, halo):
        return call(
            unpack_field(halo),
            [struct(*block), struct(halo, 8, 8, NY), struct(halo, 8, 8, NY)],
            [SMEM] + [ANY] * CHIPS,
            [VMEM] * 3,
            [pltpu.VMEM((2, CHIPS, 2, PLANES, ROWS, LANES), F32), DMA((2, CHIPS))],
        )(ids, *pieces)

    own_k, up, down = unpack(to_chips(pieces), HALO)
    above_k, below_k = along_chain(up, down)
    same, other, own_k = lax.optimization_barrier((same, other, own_k))
    pieces = call(
        pack_adjoint, [piece] * CHIPS, [SMEM, ANY, ANY], [VMEM] * CHIPS, [DMA((2, CHIPS))]
    )(ids, same, other)
    ends, up, down = unpack(to_chips(pieces), HALO - 1)
    above, below = along_chain(up, down)

    states, rate, own_k = lax.optimization_barrier((forward_states, coarse_rate, own_k))
    other_states = call(
        pack_states_first, struct(3, *part), [SMEM, ANY, ANY], VMEM, [DMA((3,))], 56
    )(ids, states, rate)
    other_states = lax.ppermute(other_states, "space", masks[1])
    states, rate, ends = lax.optimization_barrier((states, rate, ends))
    pieces = call(
        pack_states,
        [struct(2, 3, PLANES, ROWS, NY)] * CHIPS,
        [SMEM] + [ANY] * 3,
        [VMEM] * CHIPS,
        [DMA((4, CHIPS))],
        56,
    )(ids, states, rate, other_states)
    states, decay, up, down = call(
        unpack_states,
        [struct(2, *block), struct(*block), struct(2, 8, 8, NY), struct(2, 8, 8, NY)],
        [SMEM] + [ANY] * CHIPS,
        [VMEM] * 4,
        [pltpu.VMEM((2, CHIPS, 2, 3, PLANES, ROWS, LANES), F32), DMA((2, CHIPS))],
    )(ids, *to_chips(pieces))
    states_above, states_below = along_chain(up, down)

    late, up, down = call(
        solve(HALO - 1),
        [struct(*block), struct(HALO, 8, 8, NY), struct(HALO, 8, 8, NY)],
        [SMEM] * 2 + [ANY] * 6,
        [ANY] * 3,
        SOLVE_SCRATCH,
        40,
        10**8,
    )(ids, weights, own_k, above_k, below_k, ends, above, below)
    late_above, late_below = along_chain(up, down)
    wide = (ROWS + 2, 8, 8, NY)
    early = call(
        solve(HALO), struct(*wide), [SMEM] * 2 + [ANY] * 6, ANY, SOLVE_SCRATCH, 40, 10**8
    )(ids, weights, own_k, above_k, below_k, late, late_above, late_below)

    pieces = call(
        face_sums,
        [struct(2, ROWS, 8, NY)] * NT,
        [SMEM] + [ANY] * 9,
        [ANY] * NT,
        [
            pltpu.VMEM(wide, F32),
            pltpu.VMEM(wide, F32),
            pltpu.VMEM((2,) + wide, F32),
            pltpu.VMEM(block, F32),
            pltpu.VMEM(block, F32),
            pltpu.VMEM((2, 2, ROWS, 8, 8, LANES), F32),
            pltpu.VMEM((8, 2, ROWS, 8, NY), F32),
            DMA((9,)),
            DMA((NT,)),
        ],
        40,
    )(
        ids,
        late,
        late_above,
        late_below,
        early,
        states,
        states_above,
        states_below,
        decay,
        ends,
    )
    pieces = [
        lax.ppermute(
            pieces[step],
            both,
            [
                (t * GROUP + 2 * g + core, g * GROUP + 2 * (t ^ step) + core)
                for t in range(NT)
                for g in range(CHIPS)
                for core in range(2)
            ],
        )
        for step in range(NT)
    ]
    mine, other = call(
        recur,
        [struct(NT + 1, PLANES, ROWS, NY)] * 2,
        [SMEM] + [ANY] * (NT + 2),
        [ANY] * 2,
        [
            pltpu.VMEM((2, NT, 2, ROWS, 8, LANES), F32),
            pltpu.VMEM((2, PLANES, ROWS, NY), F32),
            pltpu.VMEM((2, NT + 1, PLANES, ROWS, NY), F32),
            DMA((2, NT)),
            DMA((2,)),
        ],
    )(ids, coarse_rate, other_states, *pieces)
    other = lax.ppermute(other, "space", masks[1])
    pieces = call(
        pack_results,
        [struct(2, PLANES, 2 * ROWS, NY)] * NT,
        [SMEM, ANY, ANY],
        [VMEM] * NT,
        [DMA((4 * NT,))],
    )(ids, mine, other)
    pieces = [pieces[0]] + [
        lax.ppermute(pieces[step], "tm", [(t, t ^ step) for t in range(NT)])
        for step in range(1, NT)
    ]
    adjoint_next, sensitivity = call(
        place_results,
        [struct(1, PLANES, NY, NY), struct(PLANES, NY, NY)],
        [SMEM] + [ANY] * NT,
        [VMEM] * 2,
        [DMA((2, NT))],
    )(ids, *pieces)
    return (adjoint_next, sensitivity)


def solution(mesh):
    return jax.shard_map(
        per_device,
        mesh=mesh,
        in_specs=(
            P("tm", "space", None, None),
            P("tm", None, "space", None, None),
            P("space", None, None),
            P("space", None, None),
            P("space", None, None),
            P(),
            P(),
        ),
        out_specs=(P("tm", "space", None, None), P("space", None, None)),
        check_vma=False,
    )
```

```python
import jax
import jax.numpy as jnp
from jax import lax
from jax.experimental import pallas as pl
from jax.experimental.pallas import tpu as pltpu
from jax.sharding import PartitionSpec as P

SWEEPS = 8
NT = 8
GROUP = 16
CHIPS = 8
PLANES = 4
ROWS = 16
NY = 256
LANES = 128
HALO = 9
UNROLL = 8
EXT = ROWS + 2 * HALO
F32 = jnp.float32
ANY = pl.BlockSpec(memory_space=pl.ANY)
SMEM = pl.BlockSpec(memory_space=pltpu.SMEM)
VMEM = pl.BlockSpec(memory_space=pltpu.VMEM)
DMA = pltpu.SemaphoreType.DMA


def chain_chip(g):
    return g ^ ((g >> 1) & 1)


def chain_place(c):
    return 2 * chain_chip(c >> 1) + (c & 1)


def call(kernel, out_shape, in_specs, out_specs, scratch, megabytes=24):
    return pl.pallas_call(
        kernel,
        out_shape=out_shape,
        in_specs=in_specs,
        out_specs=out_specs,
        scratch_shapes=scratch,
        compiler_params=pltpu.CompilerParams(vmem_limit_bytes=megabytes * 1024 * 1024),
    )


def struct(*shape):
    return jax.ShapeDtypeStruct(shape, F32)


def run(todo):
    for copy in todo:
        copy.start()
    for copy in todo:
        copy.wait()


def by_chip(field):
    return field.reshape(PLANES, CHIPS, 2, ROWS, NY)


def pack_field(field, out, sems):
    run(
        [
            pltpu.make_async_copy(
                field.at[:, pl.ds(chain_place(c) * ROWS, ROWS), :], out.at[c], sems.at[c]
            )
            for c in range(GROUP)
        ]
    )


DEPTH = 3 * PLANES * ROWS + 16
STEPS = (0, 1, 2, 6, 5, 3, 7, 4)


def state_copies(states, rate, edges, place, core, target, sems):
    rows = pl.ds(pl.multiple_of((2 * place + core) * ROWS, ROWS), ROWS)
    todo = [
        pltpu.make_async_copy(
            field.at[plane, rows, :],
            target.at[pl.ds((at * PLANES + plane) * ROWS, ROWS)],
            sems.at[at * PLANES + plane],
        )
        for at, field in enumerate((states.at[0, 1], states.at[0, 0], rate))
        for plane in range(PLANES)
    ]
    todo.append(
        pltpu.make_async_copy(
            edges.at[2 * place + core],
            target.at[pl.ds(DEPTH - 16, 16)],
            sems.at[3 * PLANES],
        )
    )
    return todo


def pack_states_first(ids, states, rate, edges, out, sems):
    todo = []
    for place in range(CHIPS):
        todo += state_copies(
            states, rate, edges, place, 1 - ids[2], out.at[place], sems.at[place]
        )
    run(todo)


def pack_states(ids, states, rate, edges, received, *refs):
    outs, sems, more = refs[:CHIPS], refs[CHIPS], refs[CHIPS + 1]
    chip, core = ids[1], ids[2]
    todo = []
    for step in range(CHIPS):
        place = chain_chip(chip ^ STEPS[step])
        todo += state_copies(
            states, rate, edges, place, core, outs[step].at[core], sems.at[step]
        )
        todo.append(
            pltpu.make_async_copy(received.at[place], outs[step].at[1 - core], more.at[step])
        )
    run(todo)


def edge_rows(states):
    blocks = states[0].reshape(2, PLANES, GROUP, ROWS, NY)
    zero = jnp.zeros((2, PLANES, 1, NY), F32)
    before = jnp.concatenate([zero, blocks[:, :, :-1, ROWS - 1]], axis=2)
    after = jnp.concatenate([blocks[:, :, 1:, 0], zero], axis=2)
    edges = jnp.stack([before[::-1], after[::-1]], axis=1)
    return edges.transpose(3, 0, 1, 2, 4).reshape(GROUP, 16, NY)


def fetch_pieces(chip, pieces, slots, sems):
    todo = []
    for step, piece in enumerate(pieces):
        for half in range(2):
            todo.append(
                pltpu.make_async_copy(
                    piece.at[:, :, pl.ds(half * LANES, LANES)],
                    slots.at[half, pl.ds(2 * (chip ^ STEPS[step]), 2)],
                    sems.at[half, step],
                )
            )
    run(todo)


def strided(flat, start, stride):
    return jnp.concatenate(
        [flat[half][pl.ds(start, 8, stride=stride), :] for half in range(2)], axis=1
    )


def halves(slots):
    size = 1
    for extent in slots.shape[1:-1]:
        size *= extent
    return [slots.at[half].reshape(size, LANES) for half in range(2)]


def fetch_halves(received, slots, sems):
    every = (slice(None),) * (len(received.shape) - 1)
    run(
        [
            pltpu.make_async_copy(
                received.at[every + (pl.ds(half * LANES, LANES),)], slots.at[half], sems.at[half]
            )
            for half in range(2)
        ]
    )


def unpack_field(halo):
    def kernel(received, own, up, down, slots, sems):
        fetch_halves(received, slots, sems)
        flat = halves(slots)

        def one_row(row, carry):
            for i in range(8):
                own[row, i] = strided(flat, i * ROWS + row, 8 * ROWS)
            return carry

        lax.fori_loop(0, ROWS, one_row, 0)
        up[...] = own[0:halo]
        down[...] = own[ROWS - halo :]

    return kernel


def lines_of(slots):
    flat = halves(slots)

    def lines(i, line):
        return strided(flat, (i // PLANES) * slots.shape[2] + line, 2 * slots.shape[2])

    return lines


def unpack_states(ids, *refs):
    pieces = refs[:CHIPS]
    own, decay, slots, sems = refs[CHIPS:]
    fetch_pieces(ids[1], pieces, slots, sems)
    lines = lines_of(slots)

    def one_row(row, carry):
        for i in range(8):
            for field in range(2):
                own[field, row + 1, i] = lines(i, (field * PLANES + i % PLANES) * ROWS + row)
            decay[row, i] = jnp.exp(-lines(i, (2 * PLANES + i % PLANES) * ROWS + row))
        return carry

    lax.fori_loop(0, ROWS, one_row, 0)
    for i in range(8):
        for field in range(2):
            for side in range(2):
                line = 3 * PLANES * ROWS + (field * 2 + side) * PLANES + i % PLANES
                own[field, side * (ROWS + 1), i] = lines(i, line)


def coefficients(weights, k, kx, ky, kw, kz, diag):
    scale = weights[0]
    half = 0.5 * scale
    rest = weights[1] - scale
    lane = lax.broadcasted_iota(jnp.int32, (8, NY), 1)
    place = lax.broadcasted_iota(jnp.int32, (8, NY), 0)

    def one_row(e, carry):
        mids = [k[e, i] for i in range(8)]
        last = pltpu.roll(mids[7], 1, 0)
        kz[e, 0] = jnp.where(place == 0, 0.0, half * (mids[0] + last))
        for i in range(8):
            mid = mids[i]
            if i:
                kz[e, i] = half * (mid + mids[i - 1])
            before = jnp.where(lane == 0, 0.0, half * (mid + pltpu.roll(mid, 1, 1)))
            behind = jnp.where(lane == NY - 1, 0.0, half * (mid + pltpu.roll(mid, NY - 1, 1)))
            x_low = half * (mid + k[e - 1, i])
            x_high = half * (mid + k[e + 1, i])
            own = half * mid
            extra = jnp.where((lane == 0) | (lane == NY - 1), own, 0.0)
            if i == 0:
                extra = extra + jnp.where(place == 0, own, 0.0)
            if i == 7:
                extra = extra + jnp.where(place == 7, own, 0.0)
            kx[e, i] = x_low
            ky[e, i] = before
            kw[e, i] = behind
            diag[e, i] = rest - extra - (before + behind) - (x_low + x_high)
        return carry

    def two_rows(n, carry):
        one_row(2 * n + 1, carry)
        one_row(2 * n + 2, carry)
        return carry

    lax.fori_loop(0, EXT // 2 - 1, two_rows, 0)
    for i in range(8):
        kx[EXT - 1, i] = half * (k[EXT - 2, i] + k[EXT - 1, i])


def sweeps(ids, first, weights, rhs, d0, d1, kx, ky, kw, kz, diag):
    at = 2 * chain_chip(ids[1]) + ids[2]
    low = jnp.where(at == 0, HALO, 0)
    high = jnp.where(at == GROUP - 1, HALO + ROWS, EXT)
    start_weight = weights[2]
    zeros = jnp.zeros((8, NY), F32)

    def opening(e, carry):
        for i in range(8):
            d0[e, i] = start_weight * rhs[e, i]
            d1[e, i] = zeros
        return carry

    lax.fori_loop(first, EXT - first, opening, 0)

    def one_sweep(step, cur, nxt):
        share = weights[3 + 2 * step]
        weight = weights[4 + 2 * step]

        def one_row(e, inner):
            v = [cur[e, i] for i in range(8)]
            head = kz[e, 0] * (v[0] - pltpu.roll(v[7], 1, 0))
            tail = pltpu.roll(head, 7, 0)
            flux = head
            for i in range(8):
                mid = v[i]
                flux_next = kz[e, i + 1] * (v[i + 1] - mid) if i < 7 else tail
                total = (
                    diag[e, i] * mid
                    + (flux_next - flux)
                    + kx[e, i] * cur[e - 1, i]
                    + kx[e + 1, i] * cur[e + 1, i]
                    + ky[e, i] * pltpu.roll(mid, 1, 1)
                    + kw[e, i] * pltpu.roll(mid, NY - 1, 1)
                )
                nxt[e, i] = share * total + (weight * rhs[e, i] - nxt[e, i])
                flux = flux_next
            return inner

        begin = jnp.maximum(first + step + 1, low)
        end = jnp.minimum(EXT - first - step - 1, high)

        def some_rows(n, inner):
            for extra in range(UNROLL):
                one_row(begin + UNROLL * n + extra, inner)
            return inner

        full = lax.div(end - begin, UNROLL)
        lax.fori_loop(0, full, some_rows, 0)
        rest = begin + UNROLL * full
        pairs = lax.div(end - rest, 2)

        def two_rows(n, inner):
            one_row(rest + 2 * n, inner)
            one_row(rest + 2 * n + 1, inner)
            return inner

        lax.fori_loop(0, pairs, two_rows, 0)
        lax.fori_loop(rest + 2 * pairs, end, one_row, 0)

    def two_sweeps(pair, carry):
        one_sweep(2 * pair, d0, d1)
        one_sweep(2 * pair + 1, d1, d0)
        return carry

    lax.fori_loop(0, SWEEPS // 2, two_sweeps, 0)


FIELD = (EXT, 8, 8, NY)
SOLVE_SCRATCH = [pltpu.VMEM(FIELD, F32) for _ in range(9)] + [DMA((6,)), DMA((3,))]


def solve(halo):
    first = HALO - halo
    last = EXT - first

    def kernel(ids, weights, own_k, above_k, below_k, own, above, below, *refs):
        outs = refs[:-11]
        k, kx, ky, kw, kz, diag, rhs, d0, d1, sems, out_sems = refs[-11:]
        mine = pl.ds(HALO, ROWS)
        fields = [
            pltpu.make_async_copy(above_k, k.at[pl.ds(0, HALO)], sems.at[0]),
            pltpu.make_async_copy(own_k, k.at[mine], sems.at[1]),
            pltpu.make_async_copy(below_k, k.at[pl.ds(HALO + ROWS, HALO)], sems.at[2]),
        ]
        sides = [
            pltpu.make_async_copy(above, rhs.at[pl.ds(first, halo)], sems.at[3]),
            pltpu.make_async_copy(own, rhs.at[mine], sems.at[4]),
            pltpu.make_async_copy(below, rhs.at[pl.ds(HALO + ROWS, halo)], sems.at[5]),
        ]
        for copy in fields + sides:
            copy.start()
        for copy in fields:
            copy.wait()
        coefficients(weights, k, kx, ky, kw, kz, diag)
        for copy in sides:
            copy.wait()
        sweeps(ids, first, weights, rhs, d0, d1, kx, ky, kw, kz, diag)
        if halo == HALO:
            todo = [pltpu.make_async_copy(d0.at[pl.ds(HALO - 1, ROWS + 2)], outs[0], out_sems.at[0])]
        else:
            todo = [
                pltpu.make_async_copy(d0.at[mine], outs[0], out_sems.at[0]),
                pltpu.make_async_copy(d0.at[pl.ds(HALO, HALO)], outs[1], out_sems.at[1]),
                pltpu.make_async_copy(d0.at[pl.ds(ROWS, HALO)], outs[2], out_sems.at[2]),
            ]
        run(todo)

    return kernel


def face_rows(w, u, field, out, add):
    lane = lax.broadcasted_iota(jnp.int32, (8, NY), 1)
    place = lax.broadcasted_iota(jnp.int32, (8, NY), 0)

    def one_row(row, carry):
        e = row + 1
        vw = [w[e, i] for i in range(8)]
        vu = [u[field, row + 1, i] for i in range(8)]
        back_w = jnp.where(place == 0, 0.0, pltpu.roll(vw[7], 1, 0))
        back_u = jnp.where(place == 0, 0.0, pltpu.roll(vu[7], 1, 0))
        head = (vw[0] - back_w) * (vu[0] - back_u)
        face = head
        for i in range(8):
            if i < 7:
                face_next = (vw[i + 1] - vw[i]) * (vu[i + 1] - vu[i])
            else:
                face_next = jnp.where(place == 7, vw[7] * vu[7], pltpu.roll(head, 7, 0))
            side_w = jnp.where(lane == 0, 0.0, pltpu.roll(vw[i], 1, 1))
            side_u = jnp.where(lane == 0, 0.0, pltpu.roll(vu[i], 1, 1))
            face_y = (vw[i] - side_w) * (vu[i] - side_u)
            far_y = jnp.where(lane == NY - 1, vw[i] * vu[i], pltpu.roll(face_y, NY - 1, 1))
            total = (
                (face + face_next)
                + (face_y + far_y)
                + (vw[i] - w[e - 1, i]) * (vu[i] - u[field, row, i])
                + (vw[i] - w[e + 1, i]) * (vu[i] - u[field, row + 2, i])
            )
            total = -0.5 * total
            if add:
                total = out[lax.rem(row, 8), 1, lax.div(row, 8), i] + total
            out[lax.rem(row, 8), 1, lax.div(row, 8), i] = total
            face = face_next
        return carry

    lax.fori_loop(0, ROWS, one_row, 0)


def face_sums(
    ids,
    late,
    late_above,
    late_below,
    early,
    states,
    decay,
    ends,
    *refs,
):
    out, w, x, u, rate_in, ends_in, sems = refs
    tm = ids[0]
    inner = pl.ds(1, ROWS)
    todo = [
        pltpu.make_async_copy(late_above.at[HALO - 1], w.at[0], sems.at[0]),
        pltpu.make_async_copy(late, w.at[inner], sems.at[1]),
        pltpu.make_async_copy(late_below.at[0], w.at[ROWS + 1], sems.at[2]),
        pltpu.make_async_copy(states, u, sems.at[3]),
        pltpu.make_async_copy(early, x, sems.at[4]),
        pltpu.make_async_copy(decay, rate_in, sems.at[5]),
        pltpu.make_async_copy(ends, ends_in, sems.at[6]),
    ]
    run(todo)
    face_rows(w, u, 0, out, False)
    face_rows(x, u, 1, out, True)
    keep = jnp.where(tm == NT - 1, 0.0, 1.0)

    def last_row(row, carry):
        for i in range(8):
            value = x[row + 1, i] - keep * (rate_in[row, i] * ends_in[row, i])
            out[lax.rem(row, 8), 0, lax.div(row, 8), i] = value
        return carry

    lax.fori_loop(0, ROWS, last_row, 0)


def recur(ids, decay, received, out, rates, lines, total, sems):
    copies = [
        pltpu.make_async_copy(decay.at[ids[0] + 8 * r], rates.at[r], sems.at[r])
        for r in range(2)
    ]
    run(copies)

    def split(value, target, index):
        for half in range(2):
            target[(half,) + index] = value[:, half * LANES : (half + 1) * LANES]

    def one_plane(i, carry):
        for r in range(2):
            rate = rates[r, i]
            value = received[NT - 1, 0, r, i]
            split(value, lines, (NT - 1, i, r))
            for slab in range(NT - 2, -1, -1):
                value = received[slab, 0, r, i] + rate * value
                split(value, lines, (slab, i, r))
            summed = received[0, 1, r, i]
            for slab in range(1, NT):
                summed = summed + received[slab, 1, r, i]
            split(summed, total, (i, r))
        return carry

    lax.fori_loop(0, 8, one_plane, 0)
    flat, flat_total = halves(lines), halves(total)
    for s in range(GROUP):
        start = (s % 2) * 64 + s // 2
        summed = strided(flat_total, start, 8)

        def one_slab(slab, carry):
            out[slab * GROUP + s, 0] = strided(flat, slab * 128 + start, 8)
            out[slab * GROUP + s, 1] = summed
            return carry

        lax.fori_loop(0, NT, one_slab, 0)


def place_results(received, adjoint, sensitivity, slots, sems):
    fetch_halves(received, slots, sems)
    flat = halves(slots)
    for c in range(GROUP):
        for r in range(2):
            rows = pl.ds(chain_place(c) * ROWS + 8 * r, 8)
            for plane in range(PLANES):
                start = c * 16 + 2 * plane + r
                adjoint[0, plane, rows, :] = strided(flat, start, 256)
                sensitivity[plane, rows, :] = strided(flat, start + 8, 256)


def sweep_weights(smallest_eig, largest_eig):
    low, high = smallest_eig[0], largest_eig[0]
    center = (high + low) / 2.0
    radius = (high - low) / 2.0
    sigma = center / radius
    second = [1.0, 2.0 * sigma]
    for _ in range(SWEEPS):
        second.append(2.0 * sigma * second[-1] - second[-2])
    norm = radius * 0.5 * (second[SWEEPS + 1] - second[SWEEPS - 1])
    parts = [2.0 * second[SWEEPS - k] / norm for k in range(SWEEPS + 1)]
    weights = [2.0 / radius, 2.0 * sigma, parts[SWEEPS]]
    for k in range(SWEEPS - 1, -1, -1):
        weights += [jnp.float32(1.0 if k else 0.5), parts[k] * (1.0 if k else 0.5)]
    return jnp.stack(weights)


def per_device(
    adjoint_iterate,
    forward_states,
    conductivity,
    coarse_rate,
    terminal_adjoint,
    smallest_eig,
    largest_eig,
):
    here = lax.axis_index("space")
    ids = jnp.stack([lax.axis_index("tm"), here // 2, here % 2]).astype(jnp.int32)
    weights = sweep_weights(smallest_eig, largest_eig)
    masks = [[(c, c ^ mask) for c in range(GROUP)] for mask in range(GROUP)]
    forward = [(chain_place(i), chain_place(i + 1)) for i in range(GROUP - 1)]
    backward = [(b, a) for a, b in forward]

    def to_chips(pieces, steps):
        return [
            lax.ppermute(piece, "space", masks[2 * step]) for piece, step in zip(pieces, steps)
        ]

    def along_chain(up, down):
        return lax.ppermute(down, "space", forward), lax.ppermute(up, "space", backward)

    block = (ROWS, 8, 8, NY)
    def spread(field):
        return call(pack_field, struct(GROUP, PLANES, ROWS, NY), [ANY], VMEM, [DMA((GROUP,))], 56)(
            field
        )

    def unpack(received, halo):
        return call(
            unpack_field(halo),
            [struct(*block), struct(halo, 8, 8, NY), struct(halo, 8, 8, NY)],
            [ANY],
            [VMEM] * 3,
            [pltpu.VMEM((2, GROUP, PLANES, ROWS, LANES), F32), DMA((2,))],
        )(received)

    first = jnp.where(lax.axis_index("tm") == 0, terminal_adjoint, adjoint_iterate[0])
    ends = lax.ppermute(first, "tm", [(t, (t - 1) % NT) for t in range(NT)])
    edges = edge_rows(forward_states)
    other = call(
        pack_states_first,
        struct(CHIPS, DEPTH, NY),
        [SMEM] + [ANY] * 3,
        VMEM,
        [DMA((CHIPS, 3 * PLANES + 1))],
        56,
    )(ids, forward_states, coarse_rate, edges)
    received = lax.all_to_all(spread(conductivity), "space", 0, 0)
    received, other = lax.optimization_barrier((received, other))
    own_k, up, down = unpack(received, HALO)
    above_k, below_k = along_chain(up, down)
    other = lax.ppermute(other, "space", masks[1])
    ends, own_k = lax.optimization_barrier((ends, own_k))
    received = lax.all_to_all(spread(ends), "space", 0, 0)
    pieces = call(
        pack_states,
        [struct(2, DEPTH, NY)] * CHIPS,
        [SMEM] + [ANY] * 4,
        [VMEM] * CHIPS,
        [DMA((CHIPS, 3 * PLANES + 1)), DMA((CHIPS,))],
        56,
    )(ids, forward_states, coarse_rate, edges, other)
    received, pieces = lax.optimization_barrier((received, list(pieces)))
    ends, up, down = unpack(received, HALO - 1)
    above, below = along_chain(up, down)
    pieces[1:5] = to_chips(pieces[1:5], STEPS[1:5])

    late, up, down = call(
        solve(HALO - 1),
        [struct(*block), struct(HALO, 8, 8, NY), struct(HALO, 8, 8, NY)],
        [SMEM] * 2 + [ANY] * 6,
        [ANY] * 3,
        SOLVE_SCRATCH,
        56,
    )(ids, weights, own_k, above_k, below_k, ends, above, below)
    pieces[1:5], late, up, down = lax.optimization_barrier((pieces[1:5], late, up, down))
    late_above, late_below = along_chain(up, down)
    pieces[5:], late_above, late_below = lax.optimization_barrier(
        (pieces[5:], late_above, late_below)
    )
    pieces[5:] = to_chips(pieces[5:], STEPS[5:])
    wide = (ROWS + 2, 8, 8, NY)
    early = call(
        solve(HALO), struct(*wide), [SMEM] * 2 + [ANY] * 6, ANY, SOLVE_SCRATCH, 56
    )(ids, weights, own_k, above_k, below_k, late, late_above, late_below)

    pieces, early = lax.optimization_barrier((pieces, early))
    states, decay = call(
        unpack_states,
        [struct(2, *wide), struct(*block)],
        [SMEM] + [ANY] * CHIPS,
        [VMEM] * 2,
        [pltpu.VMEM((2, GROUP, DEPTH, LANES), F32), DMA((2, CHIPS))],
    )(ids, *pieces)
    parts = call(
        face_sums,
        struct(NT, 2, 2, 8, 8, NY),
        [SMEM] + [ANY] * 7,
        VMEM,
        [
            pltpu.VMEM(wide, F32),
            pltpu.VMEM(wide, F32),
            pltpu.VMEM((2,) + wide, F32),
            pltpu.VMEM(block, F32),
            pltpu.VMEM(block, F32),
            DMA((7,)),
        ],
        40,
    )(
        ids,
        late,
        late_above,
        late_below,
        early,
        states,
        decay,
        ends,
    )
    parts = lax.all_to_all(parts, "tm", 0, 0)
    results = call(
        recur,
        struct(NT * GROUP, 2, 8, NY),
        [SMEM, ANY, VMEM],
        VMEM,
        [
            pltpu.VMEM((2, 8, 8, NY), F32),
            pltpu.VMEM((2, NT, 8, 2, 8, LANES), F32),
            pltpu.VMEM((2, 8, 2, 8, LANES), F32),
            DMA((2,)),
        ],
    )(ids, decay, parts)
    results = lax.all_to_all(results, ("tm", "space"), 0, 0)
    adjoint_next, sensitivity = call(
        place_results,
        [struct(1, PLANES, NY, NY), struct(PLANES, NY, NY)],
        [ANY],
        [VMEM] * 2,
        [pltpu.VMEM((2, NT * GROUP, 2, 8, LANES), F32), DMA((2,))],
    )(results)
    return (adjoint_next, sensitivity)


def solution(mesh):
    return jax.shard_map(
        per_device,
        mesh=mesh,
        in_specs=(
            P("tm", "space", None, None),
            P("tm", None, "space", None, None),
            P("space", None, None),
            P("space", None, None),
            P("space", None, None),
            P(),
            P(),
        ),
        out_specs=(P("tm", "space", None, None), P("space", None, None)),
        check_vma=False,
    )
```

```python
import jax
import jax.numpy as jnp
from jax import lax
from jax.experimental import pallas as pl
from jax.experimental.pallas import tpu as pltpu
from jax.sharding import PartitionSpec as P

SWEEPS = 8
NT = 8
GROUP = 16
CHIPS = 8
PLANES = 4
ROWS = 16
NY = 256
LANES = 128
HALO = 9
UNROLL = 8
EXT = ROWS + 2 * HALO
F32 = jnp.float32
ANY = pl.BlockSpec(memory_space=pl.ANY)
SMEM = pl.BlockSpec(memory_space=pltpu.SMEM)
VMEM = pl.BlockSpec(memory_space=pltpu.VMEM)
DMA = pltpu.SemaphoreType.DMA


def chain_chip(g):
    return g ^ ((g >> 1) & 1)


def chain_place(c):
    return 2 * chain_chip(c >> 1) + (c & 1)


def call(kernel, out_shape, in_specs, out_specs, scratch, megabytes=24):
    return pl.pallas_call(
        kernel,
        out_shape=out_shape,
        in_specs=in_specs,
        out_specs=out_specs,
        scratch_shapes=scratch,
        compiler_params=pltpu.CompilerParams(vmem_limit_bytes=megabytes * 1024 * 1024),
    )


def struct(*shape):
    return jax.ShapeDtypeStruct(shape, F32)


def run(todo):
    for copy in todo:
        copy.start()
    for copy in todo:
        copy.wait()


def by_chip(field):
    return field.reshape(PLANES, CHIPS, 2, ROWS, NY)


def pack_field(field, out, sems):
    run(
        [
            pltpu.make_async_copy(
                field.at[:, pl.ds(chain_place(c) * ROWS, ROWS), :], out.at[c], sems.at[c]
            )
            for c in range(GROUP)
        ]
    )


DEPTH = 3 * PLANES * ROWS + 16
STEPS = (0, 1, 2, 6, 5, 3, 7, 4)


def state_copies(states, rate, edges, place, core, target, sems):
    rows = pl.ds(pl.multiple_of((2 * place + core) * ROWS, ROWS), ROWS)
    todo = [
        pltpu.make_async_copy(
            field.at[plane, rows, :],
            target.at[pl.ds((at * PLANES + plane) * ROWS, ROWS)],
            sems.at[at * PLANES + plane],
        )
        for at, field in enumerate((states.at[0, 1], states.at[0, 0], rate))
        for plane in range(PLANES)
    ]
    todo.append(
        pltpu.make_async_copy(
            edges.at[2 * place + core],
            target.at[pl.ds(DEPTH - 16, 16)],
            sems.at[3 * PLANES],
        )
    )
    return todo


def pack_states_first(ids, states, rate, edges, out, sems):
    todo = []
    for place in range(CHIPS):
        todo += state_copies(
            states, rate, edges, place, 1 - ids[2], out.at[place], sems.at[place]
        )
    run(todo)


def pack_states(ids, states, rate, edges, received, *refs):
    outs, sems, more = refs[:CHIPS], refs[CHIPS], refs[CHIPS + 1]
    chip, core = ids[1], ids[2]
    todo = []
    for step in range(CHIPS):
        place = chain_chip(chip ^ STEPS[step])
        todo += state_copies(
            states, rate, edges, place, core, outs[step].at[core], sems.at[step]
        )
        todo.append(
            pltpu.make_async_copy(received.at[place], outs[step].at[1 - core], more.at[step])
        )
    run(todo)


def edge_rows(states):
    blocks = states[0].reshape(2, PLANES, GROUP, ROWS, NY)
    zero = jnp.zeros((2, PLANES, 1, NY), F32)
    before = jnp.concatenate([zero, blocks[:, :, :-1, ROWS - 1]], axis=2)
    after = jnp.concatenate([blocks[:, :, 1:, 0], zero], axis=2)
    edges = jnp.stack([before[::-1], after[::-1]], axis=1)
    return edges.transpose(3, 0, 1, 2, 4).reshape(GROUP, 16, NY)


def fetch_pieces(chip, pieces, slots, sems):
    todo = []
    for step, piece in enumerate(pieces):
        for half in range(2):
            todo.append(
                pltpu.make_async_copy(
                    piece.at[:, :, pl.ds(half * LANES, LANES)],
                    slots.at[half, pl.ds(2 * (chip ^ STEPS[step]), 2)],
                    sems.at[half, step],
                )
            )
    run(todo)


def strided(flat, start, stride):
    return jnp.concatenate(
        [flat[half][pl.ds(start, 8, stride=stride), :] for half in range(2)], axis=1
    )


def halves(slots):
    size = 1
    for extent in slots.shape[1:-1]:
        size *= extent
    return [slots.at[half].reshape(size, LANES) for half in range(2)]


def fetch_halves(received, slots, sems):
    every = (slice(None),) * (len(received.shape) - 1)
    run(
        [
            pltpu.make_async_copy(
                received.at[every + (pl.ds(half * LANES, LANES),)], slots.at[half], sems.at[half]
            )
            for half in range(2)
        ]
    )


def unpack_field(halo):
    def kernel(received, own, up, down, slots, sems):
        fetch_halves(received, slots, sems)
        flat = halves(slots)

        def one_row(row, carry):
            for i in range(8):
                own[row, i] = strided(flat, i * ROWS + row, 8 * ROWS)
            return carry

        lax.fori_loop(0, ROWS, one_row, 0)
        up[...] = own[0:halo]
        down[...] = own[ROWS - halo :]

    return kernel


def lines_of(slots):
    flat = halves(slots)

    def lines(i, line):
        return strided(flat, (i // PLANES) * slots.shape[2] + line, 2 * slots.shape[2])

    return lines


def unpack_states(ids, *refs):
    pieces = refs[:CHIPS]
    own, decay, slots, sems = refs[CHIPS:]
    fetch_pieces(ids[1], pieces, slots, sems)
    lines = lines_of(slots)

    def one_row(row, carry):
        for i in range(8):
            for field in range(2):
                own[field, row + 1, i] = lines(i, (field * PLANES + i % PLANES) * ROWS + row)
            decay[row, i] = jnp.exp(-lines(i, (2 * PLANES + i % PLANES) * ROWS + row))
        return carry

    lax.fori_loop(0, ROWS, one_row, 0)
    for i in range(8):
        for field in range(2):
            for side in range(2):
                line = 3 * PLANES * ROWS + (field * 2 + side) * PLANES + i % PLANES
                own[field, side * (ROWS + 1), i] = lines(i, line)


def coefficients(weights, k, kx, ky, kw, kz, diag):
    scale = weights[0]
    half = 0.5 * scale
    rest = weights[1] - scale
    lane = lax.broadcasted_iota(jnp.int32, (8, NY), 1)
    place = lax.broadcasted_iota(jnp.int32, (8, NY), 0)

    def one_row(e, carry):
        mids = [k[e, i] for i in range(8)]
        last = pltpu.roll(mids[7], 1, 0)
        kz[e, 0] = jnp.where(place == 0, 0.0, half * (mids[0] + last))
        for i in range(8):
            mid = mids[i]
            if i:
                kz[e, i] = half * (mid + mids[i - 1])
            before = jnp.where(lane == 0, 0.0, half * (mid + pltpu.roll(mid, 1, 1)))
            behind = jnp.where(lane == NY - 1, 0.0, half * (mid + pltpu.roll(mid, NY - 1, 1)))
            x_low = half * (mid + k[e - 1, i])
            x_high = half * (mid + k[e + 1, i])
            own = half * mid
            extra = jnp.where((lane == 0) | (lane == NY - 1), own, 0.0)
            if i == 0:
                extra = extra + jnp.where(place == 0, own, 0.0)
            if i == 7:
                extra = extra + jnp.where(place == 7, own, 0.0)
            kx[e, i] = x_low
            ky[e, i] = before
            kw[e, i] = behind
            diag[e, i] = rest - extra - (before + behind) - (x_low + x_high)
        return carry

    def two_rows(n, carry):
        one_row(2 * n + 1, carry)
        one_row(2 * n + 2, carry)
        return carry

    lax.fori_loop(0, EXT // 2 - 1, two_rows, 0)
    for i in range(8):
        kx[EXT - 1, i] = half * (k[EXT - 2, i] + k[EXT - 1, i])


def sweeps(ids, first, weights, rhs, d0, d1, kx, ky, kw, kz, diag):
    at = 2 * chain_chip(ids[1]) + ids[2]
    low = jnp.where(at == 0, HALO, 0)
    high = jnp.where(at == GROUP - 1, HALO + ROWS, EXT)
    start_weight = weights[2]
    zeros = jnp.zeros((8, NY), F32)

    def opening(e, carry):
        for i in range(8):
            d0[e, i] = start_weight * rhs[e, i]
            d1[e, i] = zeros
        return carry

    lax.fori_loop(first, EXT - first, opening, 0)

    def one_sweep(step, cur, nxt):
        share = weights[3 + 2 * step]
        weight = weights[4 + 2 * step]

        def one_row(e, inner):
            v = [cur[e, i] for i in range(8)]
            head = kz[e, 0] * (v[0] - pltpu.roll(v[7], 1, 0))
            tail = pltpu.roll(head, 7, 0)
            flux = head
            for i in range(8):
                mid = v[i]
                flux_next = kz[e, i + 1] * (v[i + 1] - mid) if i < 7 else tail
                total = (
                    diag[e, i] * mid
                    + (flux_next - flux)
                    + kx[e, i] * cur[e - 1, i]
                    + kx[e + 1, i] * cur[e + 1, i]
                    + ky[e, i] * pltpu.roll(mid, 1, 1)
                    + kw[e, i] * pltpu.roll(mid, NY - 1, 1)
                )
                nxt[e, i] = share * total + (weight * rhs[e, i] - nxt[e, i])
                flux = flux_next
            return inner

        begin = jnp.maximum(first + step + 1, low)
        end = jnp.minimum(EXT - first - step - 1, high)

        def some_rows(n, inner):
            for extra in range(UNROLL):
                one_row(begin + UNROLL * n + extra, inner)
            return inner

        full = lax.div(end - begin, UNROLL)
        lax.fori_loop(0, full, some_rows, 0)
        rest = begin + UNROLL * full
        pairs = lax.div(end - rest, 2)

        def two_rows(n, inner):
            one_row(rest + 2 * n, inner)
            one_row(rest + 2 * n + 1, inner)
            return inner

        lax.fori_loop(0, pairs, two_rows, 0)
        lax.fori_loop(rest + 2 * pairs, end, one_row, 0)

    def two_sweeps(pair, carry):
        one_sweep(2 * pair, d0, d1)
        one_sweep(2 * pair + 1, d1, d0)
        return carry

    lax.fori_loop(0, SWEEPS // 2, two_sweeps, 0)


FIELD = (EXT, 8, 8, NY)
SOLVE_SCRATCH = [pltpu.VMEM(FIELD, F32) for _ in range(9)] + [DMA((6,)), DMA((3,))]


def solve(halo):
    first = HALO - halo
    last = EXT - first

    def kernel(ids, weights, own_k, above_k, below_k, own, above, below, *refs):
        outs = refs[:-11]
        k, kx, ky, kw, kz, diag, rhs, d0, d1, sems, out_sems = refs[-11:]
        mine = pl.ds(HALO, ROWS)
        fields = [
            pltpu.make_async_copy(above_k, k.at[pl.ds(0, HALO)], sems.at[0]),
            pltpu.make_async_copy(own_k, k.at[mine], sems.at[1]),
            pltpu.make_async_copy(below_k, k.at[pl.ds(HALO + ROWS, HALO)], sems.at[2]),
        ]
        sides = [
            pltpu.make_async_copy(above, rhs.at[pl.ds(first, halo)], sems.at[3]),
            pltpu.make_async_copy(own, rhs.at[mine], sems.at[4]),
            pltpu.make_async_copy(below, rhs.at[pl.ds(HALO + ROWS, halo)], sems.at[5]),
        ]
        for copy in fields + sides:
            copy.start()
        for copy in fields:
            copy.wait()
        coefficients(weights, k, kx, ky, kw, kz, diag)
        for copy in sides:
            copy.wait()
        sweeps(ids, first, weights, rhs, d0, d1, kx, ky, kw, kz, diag)
        if halo == HALO:
            todo = [pltpu.make_async_copy(d0.at[pl.ds(HALO - 1, ROWS + 2)], outs[0], out_sems.at[0])]
        else:
            todo = [
                pltpu.make_async_copy(d0.at[mine], outs[0], out_sems.at[0]),
                pltpu.make_async_copy(d0.at[pl.ds(HALO, HALO)], outs[1], out_sems.at[1]),
                pltpu.make_async_copy(d0.at[pl.ds(ROWS, HALO)], outs[2], out_sems.at[2]),
            ]
        run(todo)

    return kernel


def face_rows(w, u, field, out, add):
    lane = lax.broadcasted_iota(jnp.int32, (8, NY), 1)
    place = lax.broadcasted_iota(jnp.int32, (8, NY), 0)

    def one_row(row, carry):
        e = row + 1
        vw = [w[e, i] for i in range(8)]
        vu = [u[field, row + 1, i] for i in range(8)]
        back_w = jnp.where(place == 0, 0.0, pltpu.roll(vw[7], 1, 0))
        back_u = jnp.where(place == 0, 0.0, pltpu.roll(vu[7], 1, 0))
        head = (vw[0] - back_w) * (vu[0] - back_u)
        face = head
        for i in range(8):
            if i < 7:
                face_next = (vw[i + 1] - vw[i]) * (vu[i + 1] - vu[i])
            else:
                face_next = jnp.where(place == 7, vw[7] * vu[7], pltpu.roll(head, 7, 0))
            side_w = jnp.where(lane == 0, 0.0, pltpu.roll(vw[i], 1, 1))
            side_u = jnp.where(lane == 0, 0.0, pltpu.roll(vu[i], 1, 1))
            face_y = (vw[i] - side_w) * (vu[i] - side_u)
            far_y = jnp.where(lane == NY - 1, vw[i] * vu[i], pltpu.roll(face_y, NY - 1, 1))
            total = (
                (face + face_next)
                + (face_y + far_y)
                + (vw[i] - w[e - 1, i]) * (vu[i] - u[field, row, i])
                + (vw[i] - w[e + 1, i]) * (vu[i] - u[field, row + 2, i])
            )
            total = -0.5 * total
            if add:
                total = out[lax.rem(row, 8), 1, lax.div(row, 8), i] + total
            out[lax.rem(row, 8), 1, lax.div(row, 8), i] = total
            face = face_next
        return carry

    lax.fori_loop(0, ROWS, one_row, 0)


def face_sums(
    ids,
    late,
    late_above,
    late_below,
    early,
    states,
    decay,
    ends,
    *refs,
):
    out, w, x, u, rate_in, ends_in, sems = refs
    tm = ids[0]
    inner = pl.ds(1, ROWS)
    todo = [
        pltpu.make_async_copy(late_above.at[HALO - 1], w.at[0], sems.at[0]),
        pltpu.make_async_copy(late, w.at[inner], sems.at[1]),
        pltpu.make_async_copy(late_below.at[0], w.at[ROWS + 1], sems.at[2]),
        pltpu.make_async_copy(states, u, sems.at[3]),
        pltpu.make_async_copy(early, x, sems.at[4]),
        pltpu.make_async_copy(decay, rate_in, sems.at[5]),
        pltpu.make_async_copy(ends, ends_in, sems.at[6]),
    ]
    run(todo)
    face_rows(w, u, 0, out, False)
    face_rows(x, u, 1, out, True)
    keep = jnp.where(tm == NT - 1, 0.0, 1.0)

    def last_row(row, carry):
        for i in range(8):
            value = x[row + 1, i] - keep * (rate_in[row, i] * ends_in[row, i])
            out[lax.rem(row, 8), 0, lax.div(row, 8), i] = value
        return carry

    lax.fori_loop(0, ROWS, last_row, 0)


def recur(ids, decay, received, out, rates, lines, total, sems):
    copies = [
        pltpu.make_async_copy(decay.at[ids[0] + 8 * r], rates.at[r], sems.at[r])
        for r in range(2)
    ]
    run(copies)

    def split(value, target, index):
        for half in range(2):
            target[(half,) + index] = value[:, half * LANES : (half + 1) * LANES]

    def one_plane(i, carry):
        for r in range(2):
            rate = rates[r, i]
            value = received[NT - 1, 0, r, i]
            split(value, lines, (NT - 1, i, r))
            for slab in range(NT - 2, -1, -1):
                value = received[slab, 0, r, i] + rate * value
                split(value, lines, (slab, i, r))
            summed = received[0, 1, r, i]
            for slab in range(1, NT):
                summed = summed + received[slab, 1, r, i]
            split(summed, total, (i, r))
        return carry

    lax.fori_loop(0, 8, one_plane, 0)
    flat, flat_total = halves(lines), halves(total)
    for s in range(GROUP):
        start = (s % 2) * 64 + s // 2
        summed = strided(flat_total, start, 8)

        def one_slab(slab, carry):
            out[slab * GROUP + s, 0] = strided(flat, slab * 128 + start, 8)
            out[slab * GROUP + s, 1] = summed
            return carry

        lax.fori_loop(0, NT, one_slab, 0)


def place_results(received, adjoint, sensitivity, slots, sems):
    fetch_halves(received, slots, sems)
    flat = halves(slots)
    for c in range(GROUP):
        for r in range(2):
            rows = pl.ds(chain_place(c) * ROWS + 8 * r, 8)
            for plane in range(PLANES):
                start = c * 16 + 2 * plane + r
                adjoint[0, plane, rows, :] = strided(flat, start, 256)
                sensitivity[plane, rows, :] = strided(flat, start + 8, 256)


def sweep_weights(smallest_eig, largest_eig):
    low, high = smallest_eig[0], largest_eig[0]
    center = (high + low) / 2.0
    radius = (high - low) / 2.0
    sigma = center / radius
    second = [1.0, 2.0 * sigma]
    for _ in range(SWEEPS):
        second.append(2.0 * sigma * second[-1] - second[-2])
    norm = radius * 0.5 * (second[SWEEPS + 1] - second[SWEEPS - 1])
    parts = [2.0 * second[SWEEPS - k] / norm for k in range(SWEEPS + 1)]
    weights = [2.0 / radius, 2.0 * sigma, parts[SWEEPS]]
    for k in range(SWEEPS - 1, -1, -1):
        weights += [jnp.float32(1.0 if k else 0.5), parts[k] * (1.0 if k else 0.5)]
    return jnp.stack(weights)


def per_device(
    adjoint_iterate,
    forward_states,
    conductivity,
    coarse_rate,
    terminal_adjoint,
    smallest_eig,
    largest_eig,
):
    here = lax.axis_index("space")
    ids = jnp.stack([lax.axis_index("tm"), here // 2, here % 2]).astype(jnp.int32)
    weights = sweep_weights(smallest_eig, largest_eig)
    masks = [[(c, c ^ mask) for c in range(GROUP)] for mask in range(GROUP)]
    forward = [(chain_place(i), chain_place(i + 1)) for i in range(GROUP - 1)]
    backward = [(b, a) for a, b in forward]

    def to_chips(pieces, steps):
        return [
            lax.ppermute(piece, "space", masks[2 * step]) for piece, step in zip(pieces, steps)
        ]

    def along_chain(up, down):
        return lax.ppermute(down, "space", forward), lax.ppermute(up, "space", backward)

    block = (ROWS, 8, 8, NY)
    def spread(field):
        return call(pack_field, struct(GROUP, PLANES, ROWS, NY), [ANY], VMEM, [DMA((GROUP,))], 56)(
            field
        )

    def unpack(received, halo):
        return call(
            unpack_field(halo),
            [struct(*block), struct(halo, 8, 8, NY), struct(halo, 8, 8, NY)],
            [ANY],
            [VMEM] * 3,
            [pltpu.VMEM((2, GROUP, PLANES, ROWS, LANES), F32), DMA((2,))],
        )(received)

    first = jnp.where(lax.axis_index("tm") == 0, terminal_adjoint, adjoint_iterate[0])
    ends = lax.ppermute(first, "tm", [(t, (t - 1) % NT) for t in range(NT)])
    edges = edge_rows(forward_states)
    other = call(
        pack_states_first,
        struct(CHIPS, DEPTH, NY),
        [SMEM] + [ANY] * 3,
        VMEM,
        [DMA((CHIPS, 3 * PLANES + 1))],
        56,
    )(ids, forward_states, coarse_rate, edges)
    conductivity, other = lax.optimization_barrier((conductivity, other))
    received = lax.all_to_all(spread(conductivity), "space", 0, 0)
    sent = spread(ends)
    received, sent = lax.optimization_barrier((received, sent))
    own_k, up, down = unpack(received, HALO)
    above_k, below_k = along_chain(up, down)
    other = lax.ppermute(other, "space", masks[1])
    received = lax.all_to_all(sent, "space", 0, 0)
    pieces = call(
        pack_states,
        [struct(2, DEPTH, NY)] * CHIPS,
        [SMEM] + [ANY] * 4,
        [VMEM] * CHIPS,
        [DMA((CHIPS, 3 * PLANES + 1)), DMA((CHIPS,))],
        56,
    )(ids, forward_states, coarse_rate, edges, other)
    received, pieces = lax.optimization_barrier((received, list(pieces)))
    ends, up, down = unpack(received, HALO - 1)
    above, below = along_chain(up, down)
    pieces[1:5] = to_chips(pieces[1:5], STEPS[1:5])

    late, up, down = call(
        solve(HALO - 1),
        [struct(*block), struct(HALO, 8, 8, NY), struct(HALO, 8, 8, NY)],
        [SMEM] * 2 + [ANY] * 6,
        [ANY] * 3,
        SOLVE_SCRATCH,
        56,
    )(ids, weights, own_k, above_k, below_k, ends, above, below)
    pieces[1:5], late, up, down = lax.optimization_barrier((pieces[1:5], late, up, down))
    late_above, late_below = along_chain(up, down)
    pieces[5:], late_above, late_below = lax.optimization_barrier(
        (pieces[5:], late_above, late_below)
    )
    pieces[5:] = to_chips(pieces[5:], STEPS[5:])
    wide = (ROWS + 2, 8, 8, NY)
    early = call(
        solve(HALO), struct(*wide), [SMEM] * 2 + [ANY] * 6, ANY, SOLVE_SCRATCH, 56
    )(ids, weights, own_k, above_k, below_k, late, late_above, late_below)

    pieces, early = lax.optimization_barrier((pieces, early))
    states, decay = call(
        unpack_states,
        [struct(2, *wide), struct(*block)],
        [SMEM] + [ANY] * CHIPS,
        [VMEM] * 2,
        [pltpu.VMEM((2, GROUP, DEPTH, LANES), F32), DMA((2, CHIPS))],
    )(ids, *pieces)
    parts = call(
        face_sums,
        struct(NT, 2, 2, 8, 8, NY),
        [SMEM] + [ANY] * 7,
        VMEM,
        [
            pltpu.VMEM(wide, F32),
            pltpu.VMEM(wide, F32),
            pltpu.VMEM((2,) + wide, F32),
            pltpu.VMEM(block, F32),
            pltpu.VMEM(block, F32),
            DMA((7,)),
        ],
        40,
    )(
        ids,
        late,
        late_above,
        late_below,
        early,
        states,
        decay,
        ends,
    )
    parts = lax.all_to_all(parts, "tm", 0, 0)
    results = call(
        recur,
        struct(NT * GROUP, 2, 8, NY),
        [SMEM, ANY, VMEM],
        VMEM,
        [
            pltpu.VMEM((2, 8, 8, NY), F32),
            pltpu.VMEM((2, NT, 8, 2, 8, LANES), F32),
            pltpu.VMEM((2, 8, 2, 8, LANES), F32),
            DMA((2,)),
        ],
    )(ids, decay, parts)
    results = lax.all_to_all(results, ("tm", "space"), 0, 0)
    adjoint_next, sensitivity = call(
        place_results,
        [struct(1, PLANES, NY, NY), struct(PLANES, NY, NY)],
        [ANY],
        [VMEM] * 2,
        [pltpu.VMEM((2, NT * GROUP, 2, 8, LANES), F32), DMA((2,))],
    )(results)
    return (adjoint_next, sensitivity)


def solution(mesh):
    return jax.shard_map(
        per_device,
        mesh=mesh,
        in_specs=(
            P("tm", "space", None, None),
            P("tm", None, "space", None, None),
            P("space", None, None),
            P("space", None, None),
            P("space", None, None),
            P(),
            P(),
        ),
        out_specs=(P("tm", "space", None, None), P("space", None, None)),
        check_vma=False,
    )
```

```python
import jax
import jax.numpy as jnp
from jax import lax
from jax.experimental import pallas as pl
from jax.experimental.pallas import tpu as pltpu
from jax.sharding import PartitionSpec as P

SWEEPS = 8
NT = 8
GROUP = 16
CHIPS = 8
PLANES = 4
ROWS = 16
NY = 256
LANES = 128
HALO = 9
UNROLL = 8
EXT = ROWS + 2 * HALO
F32 = jnp.float32
ANY = pl.BlockSpec(memory_space=pl.ANY)
SMEM = pl.BlockSpec(memory_space=pltpu.SMEM)
VMEM = pl.BlockSpec(memory_space=pltpu.VMEM)
DMA = pltpu.SemaphoreType.DMA


def chain_chip(g):
    return g ^ ((g >> 1) & 1)


def chain_place(c):
    return 2 * chain_chip(c >> 1) + (c & 1)


def call(kernel, out_shape, in_specs, out_specs, scratch, megabytes=24):
    return pl.pallas_call(
        kernel,
        out_shape=out_shape,
        in_specs=in_specs,
        out_specs=out_specs,
        scratch_shapes=scratch,
        compiler_params=pltpu.CompilerParams(vmem_limit_bytes=megabytes * 1024 * 1024),
    )


def struct(*shape):
    return jax.ShapeDtypeStruct(shape, F32)


def run(todo):
    for copy in todo:
        copy.start()
    for copy in todo:
        copy.wait()


def by_chip(field):
    return field.reshape(PLANES, CHIPS, 2, ROWS, NY)


def pack_field(field, out, sems):
    run(
        [
            pltpu.make_async_copy(
                field.at[:, pl.ds(chain_place(c) * ROWS, ROWS), :], out.at[c], sems.at[c]
            )
            for c in range(GROUP)
        ]
    )


DEPTH = 3 * PLANES * ROWS + 16
STEPS = (0, 2, 6, 4, 1, 5, 3, 7)


def state_copies(states, rate, edges, place, core, target, sems):
    rows = pl.ds(pl.multiple_of((2 * place + core) * ROWS, ROWS), ROWS)
    todo = [
        pltpu.make_async_copy(
            field.at[plane, rows, :],
            target.at[pl.ds((at * PLANES + plane) * ROWS, ROWS)],
            sems.at[at * PLANES + plane],
        )
        for at, field in enumerate((states.at[0, 1], states.at[0, 0], rate))
        for plane in range(PLANES)
    ]
    todo.append(
        pltpu.make_async_copy(
            edges.at[2 * place + core],
            target.at[pl.ds(DEPTH - 16, 16)],
            sems.at[3 * PLANES],
        )
    )
    return todo


def pack_states_first(ids, states, rate, edges, out, sems):
    todo = []
    for place in range(CHIPS):
        todo += state_copies(
            states, rate, edges, place, 1 - ids[2], out.at[place], sems.at[place]
        )
    run(todo)


def pack_states(ids, states, rate, edges, received, *refs):
    outs, sems, more = refs[:CHIPS], refs[CHIPS], refs[CHIPS + 1]
    chip, core = ids[1], ids[2]
    todo = []
    for step in range(CHIPS):
        place = chain_chip(chip ^ STEPS[step])
        todo += state_copies(
            states, rate, edges, place, core, outs[step].at[core], sems.at[step]
        )
        todo.append(
            pltpu.make_async_copy(received.at[place], outs[step].at[1 - core], more.at[step])
        )
    run(todo)


def edge_rows(states):
    blocks = states[0].reshape(2, PLANES, GROUP, ROWS, NY)
    zero = jnp.zeros((2, PLANES, 1, NY), F32)
    before = jnp.concatenate([zero, blocks[:, :, :-1, ROWS - 1]], axis=2)
    after = jnp.concatenate([blocks[:, :, 1:, 0], zero], axis=2)
    edges = jnp.stack([before[::-1], after[::-1]], axis=1)
    return edges.transpose(3, 0, 1, 2, 4).reshape(GROUP, 16, NY)


def fetch_pieces(chip, pieces, slots, sems):
    todo = []
    for step, piece in enumerate(pieces):
        for half in range(2):
            todo.append(
                pltpu.make_async_copy(
                    piece.at[:, :, pl.ds(half * LANES, LANES)],
                    slots.at[half, pl.ds(2 * (chip ^ STEPS[step]), 2)],
                    sems.at[half, step],
                )
            )
    run(todo)


def strided(flat, start, stride):
    return jnp.concatenate(
        [flat[half][pl.ds(start, 8, stride=stride), :] for half in range(2)], axis=1
    )


def halves(slots):
    size = 1
    for extent in slots.shape[1:-1]:
        size *= extent
    return [slots.at[half].reshape(size, LANES) for half in range(2)]


def fetch_halves(received, slots, sems):
    every = (slice(None),) * (len(received.shape) - 1)
    run(
        [
            pltpu.make_async_copy(
                received.at[every + (pl.ds(half * LANES, LANES),)], slots.at[half], sems.at[half]
            )
            for half in range(2)
        ]
    )


def unpack_field(halo):
    def kernel(received, own, up, down, slots, sems):
        fetch_halves(received, slots, sems)
        flat = halves(slots)

        def one_row(row, carry):
            for i in range(8):
                own[row, i] = strided(flat, i * ROWS + row, 8 * ROWS)
            return carry

        lax.fori_loop(0, ROWS, one_row, 0)
        up[...] = own[0:halo]
        down[...] = own[ROWS - halo :]

    return kernel


def lines_of(slots):
    flat = halves(slots)

    def lines(i, line):
        return strided(flat, (i // PLANES) * slots.shape[2] + line, 2 * slots.shape[2])

    return lines


def unpack_states(ids, *refs):
    pieces = refs[:CHIPS]
    own, decay, slots, sems = refs[CHIPS:]
    fetch_pieces(ids[1], pieces, slots, sems)
    lines = lines_of(slots)

    def one_row(row, carry):
        for i in range(8):
            for field in range(2):
                own[field, row + 1, i] = lines(i, (field * PLANES + i % PLANES) * ROWS + row)
            decay[row, i] = jnp.exp(-lines(i, (2 * PLANES + i % PLANES) * ROWS + row))
        return carry

    lax.fori_loop(0, ROWS, one_row, 0)
    for i in range(8):
        for field in range(2):
            for side in range(2):
                line = 3 * PLANES * ROWS + (field * 2 + side) * PLANES + i % PLANES
                own[field, side * (ROWS + 1), i] = lines(i, line)


def coefficients(weights, k, kx, ky, kw, kz, diag):
    scale = weights[0]
    half = 0.5 * scale
    rest = weights[1] - scale
    lane = lax.broadcasted_iota(jnp.int32, (8, NY), 1)
    place = lax.broadcasted_iota(jnp.int32, (8, NY), 0)

    def one_row(e, carry):
        mids = [k[e, i] for i in range(8)]
        last = pltpu.roll(mids[7], 1, 0)
        kz[e, 0] = jnp.where(place == 0, 0.0, half * (mids[0] + last))
        for i in range(8):
            mid = mids[i]
            if i:
                kz[e, i] = half * (mid + mids[i - 1])
            before = jnp.where(lane == 0, 0.0, half * (mid + pltpu.roll(mid, 1, 1)))
            behind = jnp.where(lane == NY - 1, 0.0, half * (mid + pltpu.roll(mid, NY - 1, 1)))
            x_low = half * (mid + k[e - 1, i])
            x_high = half * (mid + k[e + 1, i])
            own = half * mid
            extra = jnp.where((lane == 0) | (lane == NY - 1), own, 0.0)
            if i == 0:
                extra = extra + jnp.where(place == 0, own, 0.0)
            if i == 7:
                extra = extra + jnp.where(place == 7, own, 0.0)
            kx[e, i] = x_low
            ky[e, i] = before
            kw[e, i] = behind
            diag[e, i] = rest - extra - (before + behind) - (x_low + x_high)
        return carry

    def two_rows(n, carry):
        one_row(2 * n + 1, carry)
        one_row(2 * n + 2, carry)
        return carry

    lax.fori_loop(0, EXT // 2 - 1, two_rows, 0)
    for i in range(8):
        kx[EXT - 1, i] = half * (k[EXT - 2, i] + k[EXT - 1, i])


def sweeps(ids, first, weights, rhs, d0, d1, kx, ky, kw, kz, diag):
    at = 2 * chain_chip(ids[1]) + ids[2]
    low = jnp.where(at == 0, HALO, 0)
    high = jnp.where(at == GROUP - 1, HALO + ROWS, EXT)
    start_weight = weights[2]
    zeros = jnp.zeros((8, NY), F32)

    def opening(e, carry):
        for i in range(8):
            d0[e, i] = start_weight * rhs[e, i]
            d1[e, i] = zeros
        return carry

    lax.fori_loop(first, EXT - first, opening, 0)

    def one_sweep(step, cur, nxt):
        share = weights[3 + 2 * step]
        weight = weights[4 + 2 * step]

        def one_row(e, inner):
            v = [cur[e, i] for i in range(8)]
            head = kz[e, 0] * (v[0] - pltpu.roll(v[7], 1, 0))
            tail = pltpu.roll(head, 7, 0)
            flux = head
            for i in range(8):
                mid = v[i]
                flux_next = kz[e, i + 1] * (v[i + 1] - mid) if i < 7 else tail
                total = (
                    diag[e, i] * mid
                    + (flux_next - flux)
                    + kx[e, i] * cur[e - 1, i]
                    + kx[e + 1, i] * cur[e + 1, i]
                    + ky[e, i] * pltpu.roll(mid, 1, 1)
                    + kw[e, i] * pltpu.roll(mid, NY - 1, 1)
                )
                nxt[e, i] = share * total + (weight * rhs[e, i] - nxt[e, i])
                flux = flux_next
            return inner

        begin = jnp.maximum(first + step + 1, low)
        end = jnp.minimum(EXT - first - step - 1, high)

        def some_rows(n, inner):
            for extra in range(UNROLL):
                one_row(begin + UNROLL * n + extra, inner)
            return inner

        full = lax.div(end - begin, UNROLL)
        lax.fori_loop(0, full, some_rows, 0)
        rest = begin + UNROLL * full
        pairs = lax.div(end - rest, 2)

        def two_rows(n, inner):
            one_row(rest + 2 * n, inner)
            one_row(rest + 2 * n + 1, inner)
            return inner

        lax.fori_loop(0, pairs, two_rows, 0)
        lax.fori_loop(rest + 2 * pairs, end, one_row, 0)

    def two_sweeps(pair, carry):
        one_sweep(2 * pair, d0, d1)
        one_sweep(2 * pair + 1, d1, d0)
        return carry

    lax.fori_loop(0, SWEEPS // 2, two_sweeps, 0)


FIELD = (EXT, 8, 8, NY)
SOLVE_SCRATCH = [pltpu.VMEM(FIELD, F32) for _ in range(9)] + [DMA((6,)), DMA((3,))]


def solve(halo):
    first = HALO - halo
    last = EXT - first

    def kernel(ids, weights, own_k, above_k, below_k, own, above, below, *refs):
        outs = refs[:-11]
        k, kx, ky, kw, kz, diag, rhs, d0, d1, sems, out_sems = refs[-11:]
        mine = pl.ds(HALO, ROWS)
        fields = [
            pltpu.make_async_copy(above_k, k.at[pl.ds(0, HALO)], sems.at[0]),
            pltpu.make_async_copy(own_k, k.at[mine], sems.at[1]),
            pltpu.make_async_copy(below_k, k.at[pl.ds(HALO + ROWS, HALO)], sems.at[2]),
        ]
        sides = [
            pltpu.make_async_copy(above, rhs.at[pl.ds(first, halo)], sems.at[3]),
            pltpu.make_async_copy(own, rhs.at[mine], sems.at[4]),
            pltpu.make_async_copy(below, rhs.at[pl.ds(HALO + ROWS, halo)], sems.at[5]),
        ]
        for copy in fields + sides:
            copy.start()
        for copy in fields:
            copy.wait()
        coefficients(weights, k, kx, ky, kw, kz, diag)
        for copy in sides:
            copy.wait()
        sweeps(ids, first, weights, rhs, d0, d1, kx, ky, kw, kz, diag)
        if halo == HALO:
            todo = [pltpu.make_async_copy(d0.at[pl.ds(HALO - 1, ROWS + 2)], outs[0], out_sems.at[0])]
        else:
            todo = [
                pltpu.make_async_copy(d0.at[mine], outs[0], out_sems.at[0]),
                pltpu.make_async_copy(d0.at[pl.ds(HALO, HALO)], outs[1], out_sems.at[1]),
                pltpu.make_async_copy(d0.at[pl.ds(ROWS, HALO)], outs[2], out_sems.at[2]),
            ]
        run(todo)

    return kernel


def face_rows(w, u, field, out, add):
    lane = lax.broadcasted_iota(jnp.int32, (8, NY), 1)
    place = lax.broadcasted_iota(jnp.int32, (8, NY), 0)

    def one_row(row, carry):
        e = row + 1
        vw = [w[e, i] for i in range(8)]
        vu = [u[field, row + 1, i] for i in range(8)]
        back_w = jnp.where(place == 0, 0.0, pltpu.roll(vw[7], 1, 0))
        back_u = jnp.where(place == 0, 0.0, pltpu.roll(vu[7], 1, 0))
        head = (vw[0] - back_w) * (vu[0] - back_u)
        face = head
        for i in range(8):
            if i < 7:
                face_next = (vw[i + 1] - vw[i]) * (vu[i + 1] - vu[i])
            else:
                face_next = jnp.where(place == 7, vw[7] * vu[7], pltpu.roll(head, 7, 0))
            side_w = jnp.where(lane == 0, 0.0, pltpu.roll(vw[i], 1, 1))
            side_u = jnp.where(lane == 0, 0.0, pltpu.roll(vu[i], 1, 1))
            face_y = (vw[i] - side_w) * (vu[i] - side_u)
            far_y = jnp.where(lane == NY - 1, vw[i] * vu[i], pltpu.roll(face_y, NY - 1, 1))
            total = (
                (face + face_next)
                + (face_y + far_y)
                + (vw[i] - w[e - 1, i]) * (vu[i] - u[field, row, i])
                + (vw[i] - w[e + 1, i]) * (vu[i] - u[field, row + 2, i])
            )
            total = -0.5 * total
            if add:
                total = out[lax.rem(row, 8), 1, lax.div(row, 8), i] + total
            out[lax.rem(row, 8), 1, lax.div(row, 8), i] = total
            face = face_next
        return carry

    lax.fori_loop(0, ROWS, one_row, 0)


def face_sums(
    ids,
    late,
    late_above,
    late_below,
    early,
    states,
    decay,
    ends,
    *refs,
):
    out, w, x, u, rate_in, ends_in, sems = refs
    tm = ids[0]
    inner = pl.ds(1, ROWS)
    todo = [
        pltpu.make_async_copy(late_above.at[HALO - 1], w.at[0], sems.at[0]),
        pltpu.make_async_copy(late, w.at[inner], sems.at[1]),
        pltpu.make_async_copy(late_below.at[0], w.at[ROWS + 1], sems.at[2]),
        pltpu.make_async_copy(states, u, sems.at[3]),
        pltpu.make_async_copy(early, x, sems.at[4]),
        pltpu.make_async_copy(decay, rate_in, sems.at[5]),
        pltpu.make_async_copy(ends, ends_in, sems.at[6]),
    ]
    run(todo)
    face_rows(w, u, 0, out, False)
    face_rows(x, u, 1, out, True)
    keep = jnp.where(tm == NT - 1, 0.0, 1.0)

    def last_row(row, carry):
        for i in range(8):
            value = x[row + 1, i] - keep * (rate_in[row, i] * ends_in[row, i])
            out[lax.rem(row, 8), 0, lax.div(row, 8), i] = value
        return carry

    lax.fori_loop(0, ROWS, last_row, 0)


def recur(ids, decay, received, out, rates, lines, total, sems):
    copies = [
        pltpu.make_async_copy(decay.at[ids[0] + 8 * r], rates.at[r], sems.at[r])
        for r in range(2)
    ]
    run(copies)

    def split(value, target, index):
        for half in range(2):
            target[(half,) + index] = value[:, half * LANES : (half + 1) * LANES]

    def one_plane(i, carry):
        for r in range(2):
            rate = rates[r, i]
            value = received[NT - 1, 0, r, i]
            split(value, lines, (NT - 1, i, r))
            for slab in range(NT - 2, -1, -1):
                value = received[slab, 0, r, i] + rate * value
                split(value, lines, (slab, i, r))
            summed = received[0, 1, r, i]
            for slab in range(1, NT):
                summed = summed + received[slab, 1, r, i]
            split(summed, total, (i, r))
        return carry

    lax.fori_loop(0, 8, one_plane, 0)
    flat, flat_total = halves(lines), halves(total)
    for s in range(GROUP):
        start = (s % 2) * 64 + s // 2
        summed = strided(flat_total, start, 8)

        def one_slab(slab, carry):
            out[slab * GROUP + s, 0] = strided(flat, slab * 128 + start, 8)
            out[slab * GROUP + s, 1] = summed
            return carry

        lax.fori_loop(0, NT, one_slab, 0)


def place_results(received, adjoint, sensitivity, slots, sems):
    fetch_halves(received, slots, sems)
    flat = halves(slots)
    for c in range(GROUP):
        for r in range(2):
            rows = pl.ds(chain_place(c) * ROWS + 8 * r, 8)
            for plane in range(PLANES):
                start = c * 16 + 2 * plane + r
                adjoint[0, plane, rows, :] = strided(flat, start, 256)
                sensitivity[plane, rows, :] = strided(flat, start + 8, 256)


def sweep_weights(smallest_eig, largest_eig):
    low, high = smallest_eig[0], largest_eig[0]
    center = (high + low) / 2.0
    radius = (high - low) / 2.0
    sigma = center / radius
    second = [1.0, 2.0 * sigma]
    for _ in range(SWEEPS):
        second.append(2.0 * sigma * second[-1] - second[-2])
    norm = radius * 0.5 * (second[SWEEPS + 1] - second[SWEEPS - 1])
    parts = [2.0 * second[SWEEPS - k] / norm for k in range(SWEEPS + 1)]
    weights = [2.0 / radius, 2.0 * sigma, parts[SWEEPS]]
    for k in range(SWEEPS - 1, -1, -1):
        weights += [jnp.float32(1.0 if k else 0.5), parts[k] * (1.0 if k else 0.5)]
    return jnp.stack(weights)


def per_device(
    adjoint_iterate,
    forward_states,
    conductivity,
    coarse_rate,
    terminal_adjoint,
    smallest_eig,
    largest_eig,
):
    here = lax.axis_index("space")
    ids = jnp.stack([lax.axis_index("tm"), here // 2, here % 2]).astype(jnp.int32)
    weights = sweep_weights(smallest_eig, largest_eig)
    masks = [[(c, c ^ mask) for c in range(GROUP)] for mask in range(GROUP)]
    forward = [(chain_place(i), chain_place(i + 1)) for i in range(GROUP - 1)]
    backward = [(b, a) for a, b in forward]

    def to_chips(pieces, steps):
        return [
            lax.ppermute(piece, "space", masks[2 * step]) for piece, step in zip(pieces, steps)
        ]

    def along_chain(up, down):
        return lax.ppermute(down, "space", forward), lax.ppermute(up, "space", backward)

    block = (ROWS, 8, 8, NY)
    def spread(field):
        return call(pack_field, struct(GROUP, PLANES, ROWS, NY), [ANY], VMEM, [DMA((GROUP,))], 56)(
            field
        )

    def unpack(received, halo):
        return call(
            unpack_field(halo),
            [struct(*block), struct(halo, 8, 8, NY), struct(halo, 8, 8, NY)],
            [ANY],
            [VMEM] * 3,
            [pltpu.VMEM((2, GROUP, PLANES, ROWS, LANES), F32), DMA((2,))],
        )(received)

    first = jnp.where(lax.axis_index("tm") == 0, terminal_adjoint, adjoint_iterate[0])
    ends = lax.ppermute(first, "tm", [(t, (t - 1) % NT) for t in range(NT)])
    edges = edge_rows(forward_states)
    other = call(
        pack_states_first,
        struct(CHIPS, DEPTH, NY),
        [SMEM] + [ANY] * 3,
        VMEM,
        [DMA((CHIPS, 3 * PLANES + 1))],
        56,
    )(ids, forward_states, coarse_rate, edges)
    conductivity, other = lax.optimization_barrier((conductivity, other))
    received = lax.all_to_all(spread(conductivity), "space", 0, 0)
    sent = spread(ends)
    received, sent = lax.optimization_barrier((received, sent))
    own_k, up, down = unpack(received, HALO)
    above_k, below_k = along_chain(up, down)
    other = lax.ppermute(other, "space", masks[1])
    received = lax.all_to_all(sent, "space", 0, 0)
    pieces = call(
        pack_states,
        [struct(2, DEPTH, NY)] * CHIPS,
        [SMEM] + [ANY] * 4,
        [VMEM] * CHIPS,
        [DMA((CHIPS, 3 * PLANES + 1)), DMA((CHIPS,))],
        56,
    )(ids, forward_states, coarse_rate, edges, other)
    received, pieces = lax.optimization_barrier((received, list(pieces)))
    ends, up, down = unpack(received, HALO - 1)
    above, below = along_chain(up, down)
    pieces[1:5] = to_chips(pieces[1:5], STEPS[1:5])

    late, up, down = call(
        solve(HALO - 1),
        [struct(*block), struct(HALO, 8, 8, NY), struct(HALO, 8, 8, NY)],
        [SMEM] * 2 + [ANY] * 6,
        [ANY] * 3,
        SOLVE_SCRATCH,
        56,
    )(ids, weights, own_k, above_k, below_k, ends, above, below)
    pieces[1:5], late, up, down = lax.optimization_barrier((pieces[1:5], late, up, down))
    late_above, late_below = along_chain(up, down)
    pieces[5:], late_above, late_below = lax.optimization_barrier(
        (pieces[5:], late_above, late_below)
    )
    pieces[5:] = to_chips(pieces[5:], STEPS[5:])
    wide = (ROWS + 2, 8, 8, NY)
    early = call(
        solve(HALO), struct(*wide), [SMEM] * 2 + [ANY] * 6, ANY, SOLVE_SCRATCH, 56
    )(ids, weights, own_k, above_k, below_k, late, late_above, late_below)

    pieces, early = lax.optimization_barrier((pieces, early))
    states, decay = call(
        unpack_states,
        [struct(2, *wide), struct(*block)],
        [SMEM] + [ANY] * CHIPS,
        [VMEM] * 2,
        [pltpu.VMEM((2, GROUP, DEPTH, LANES), F32), DMA((2, CHIPS))],
    )(ids, *pieces)
    parts = call(
        face_sums,
        struct(NT, 2, 2, 8, 8, NY),
        [SMEM] + [ANY] * 7,
        VMEM,
        [
            pltpu.VMEM(wide, F32),
            pltpu.VMEM(wide, F32),
            pltpu.VMEM((2,) + wide, F32),
            pltpu.VMEM(block, F32),
            pltpu.VMEM(block, F32),
            DMA((7,)),
        ],
        40,
    )(
        ids,
        late,
        late_above,
        late_below,
        early,
        states,
        decay,
        ends,
    )
    parts = lax.all_to_all(parts, "tm", 0, 0)
    results = call(
        recur,
        struct(NT * GROUP, 2, 8, NY),
        [SMEM, ANY, VMEM],
        VMEM,
        [
            pltpu.VMEM((2, 8, 8, NY), F32),
            pltpu.VMEM((2, NT, 8, 2, 8, LANES), F32),
            pltpu.VMEM((2, 8, 2, 8, LANES), F32),
            DMA((2,)),
        ],
    )(ids, decay, parts)
    results = lax.all_to_all(results, ("tm", "space"), 0, 0)
    adjoint_next, sensitivity = call(
        place_results,
        [struct(1, PLANES, NY, NY), struct(PLANES, NY, NY)],
        [ANY],
        [VMEM] * 2,
        [pltpu.VMEM((2, NT * GROUP, 2, 8, LANES), F32), DMA((2,))],
    )(results)
    return (adjoint_next, sensitivity)


def solution(mesh):
    return jax.shard_map(
        per_device,
        mesh=mesh,
        in_specs=(
            P("tm", "space", None, None),
            P("tm", None, "space", None, None),
            P("space", None, None),
            P("space", None, None),
            P("space", None, None),
            P(),
            P(),
        ),
        out_specs=(P("tm", "space", None, None), P("space", None, None)),
        check_vma=False,
    )
```
